32 devices in a mesh: dp: 4 (over y, x), mp: 8 (over z, core).
Axes of the slice: x: 2, y: 2, z: 4, core: 2. Of those that a mesh axis runs over, the one named last changes fastest.
Arguments:
- tokens: bfloat16 [2048, 8192], P(('dp', 'mp')), may hold values from -6 to 6
- row_counts: int32 [4, 8], replicated, may hold values from 8 to 64, as said below
- gate_blocks: bfloat16 [64, 16, 128, 256], P('mp'), may hold values from -0.125 to 0.125
- gate_index: int32 [64, 16], P('mp'), may hold values from 0 to 63, as said below
- up_blocks: bfloat16 [64, 16, 128, 256], P('mp'), may hold values from -0.125 to 0.125
- up_index: int32 [64, 16], P('mp'), may hold values from 0 to 63, as said below
- down_blocks: bfloat16 [64, 16, 256, 128], P('mp'), may hold values from -0.09375 to 0.09375
- down_index: int32 [64, 16], P('mp'), may hold values from 0 to 63, as said below
Outputs:
- layer_out: bfloat16 [2048, 8192], P(('dp', 'mp'))
The draws below stay inside these ranges and needn't reach their ends.
Inputs may be any that keep to these rules, and one draw needn't show every extreme that they name: `row_counts`: every entry is a multiple of 8; the entries of one column (one mp index) add up to 32 times the number of dp indices, and every column holds one entry equal to 64. `gate_index`: each row holds 16 distinct block rows in increasing order. `up_index`: each row holds 16 distinct block rows in increasing order. `down_index`: each row holds 16 distinct block columns in increasing order.
All inputs are finite; a program needn't handle non-finite values.
Results may differ from the reference program's by a relative error of at most 0.013.
Values may be sent and summed in bfloat16 or wider, within the bound.
A program may use at most 192 MiB of HBM per device.

```python
import jax
import jax.numpy as jnp
from jax import lax

D = 8192
FF = 16384
NBD = 64
NBF = 64
KNZ = 16
ROWS_IN = 64
BD = 128
BF = 256
BAL = 32
ROWS = 2048
N_DP = 4
N_MP = 8


def pick_blocks(key):
    key_list = jax.random.split(key, NBF)

    def one_column(column_key):
        return jnp.sort(jax.random.permutation(column_key, NBD)[:KNZ])
    return jax.vmap(one_column)(key_list).astype(jnp.int32)


def draw_gate_index(key, part):
    return pick_blocks(jax.random.fold_in(key, 101))


def draw_up_index(key, part):
    return pick_blocks(jax.random.fold_in(key, 202))


def draw_down_index(key, part):
    return pick_blocks(jax.random.fold_in(key, 303))


def draw_row_counts(key, part):
    longest = ROWS_IN // 8
    target = N_DP * ROWS_IN // 16
    spare_units = target - N_DP - longest + 1
    per_device = longest - 1
    slot_total = N_DP * per_device
    owner_ids = jnp.arange(slot_total, dtype=jnp.int32) // per_device
    lane_ids = jnp.arange(N_DP, dtype=jnp.int32)

    def one_lane(lane_key):
        first_key, second_key = jax.random.split(lane_key)
        chosen = jax.random.randint(first_key, (), 0, N_DP)
        scores = jax.random.permutation(second_key, slot_total).astype(jnp.int32)
        scores = jnp.where(owner_ids == chosen, jnp.arange(slot_total, dtype=jnp.int32) - slot_total, scores)
        rank_list = jnp.argsort(jnp.argsort(scores, stable=True), stable=True)
        marked = rank_list < spare_units + per_device
        unit_count = 1 + jnp.sum(((owner_ids[None, :] == lane_ids[:, None]) & marked[None, :]).astype(jnp.int32), axis=1)
        return (8 * unit_count).astype(jnp.int32)
    key_list = jax.random.split(jax.random.fold_in(key, 404), N_MP)
    return jnp.transpose(jax.vmap(one_lane)(key_list)).astype(jnp.int32)


def level_of(rng, shape, shards, smallest, largest):
    factor_of, own = 1.0, jax.random.fold_in(rng, 6)
    for axis_at, blocks in shards:
        draws = jnp.exp(jax.random.uniform(jax.random.fold_in(own, axis_at), (blocks,), jnp.float32, smallest / len(shards), largest / len(shards)))
        factor_of = factor_of * jnp.repeat(draws, shape[axis_at] // blocks).reshape([-1 if axis == axis_at else 1 for axis in range(len(shape))])
    return factor_of


def bell_draw(stream_key, dims, deviation, most, cuts=(), kind=jnp.bfloat16):
    array = jax.random.normal(stream_key, dims, jnp.float32) * deviation
    if len(cuts) > 0:
        array = level_of(stream_key, dims, cuts, -0.22, 0.18) * array
    return jnp.clip(array, min=-most, max=most).astype(kind)


def setup_inputs(seed: int = 0) -> dict:
    splits = jax.random.split(jax.random.key(seed), 9)
    tokens = bell_draw(splits[0], (ROWS, D), 1.0, 6.0, ((0, 32),))
    row_counts = draw_row_counts(jax.random.fold_in(splits[8], 71), 0)
    gate_blocks = bell_draw(splits[2], (NBF, KNZ, BD, BF), (KNZ * BD) ** -0.5, 0.125, ((0, 8),))
    gate_index = draw_gate_index(jax.random.fold_in(splits[8], 71), 0)
    up_blocks = bell_draw(splits[4], (NBF, KNZ, BD, BF), (KNZ * BD) ** -0.5, 0.125, ((0, 8),))
    up_index = draw_up_index(jax.random.fold_in(splits[8], 71), 0)
    down_blocks = bell_draw(splits[6], (NBF, KNZ, BF, BD), (FF * KNZ // NBD) ** -0.5, 0.09375, ((0, 8),))
    down_index = draw_down_index(jax.random.fold_in(splits[8], 71), 0)
    return {"tokens": tokens, "row_counts": row_counts, "gate_blocks": gate_blocks, "gate_index": gate_index, "up_blocks": up_blocks, "up_index": up_index, "down_blocks": down_blocks, "down_index": down_index}


def make_hidden(row_block, gate_blocks, gate_index, up_blocks, up_index):
    row_count = row_block.shape[0]
    split_rows = row_block.reshape(row_count, NBD, BD).astype(jnp.float32)
    gate_input = jnp.take(split_rows, gate_index, axis=1)
    up_input = jnp.take(split_rows, up_index, axis=1)
    gate_value = jnp.einsum("rjkc,jkcn->rjn", gate_input, gate_blocks.astype(jnp.float32), precision=lax.Precision.HIGHEST)
    up_value = jnp.einsum("rjkc,jkcn->rjn", up_input, up_blocks.astype(jnp.float32), precision=lax.Precision.HIGHEST)
    return (jax.nn.silu(gate_value) * up_value).astype(jnp.bfloat16)


def apply_down(hidden, down_blocks, down_index):
    products = jnp.einsum("rjn,jknc->rjkc", hidden.astype(jnp.float32), down_blocks.astype(jnp.float32), precision=lax.Precision.HIGHEST)
    placing = (down_index[:, :, None] == jnp.arange(NBD, dtype=jnp.int32)[None, None, :]).astype(jnp.float32)
    placed = jnp.einsum("rjkc,jkd->rdc", products, placing, precision=lax.Precision.HIGHEST)
    return placed.reshape(hidden.shape[0], D)


def reference(tokens, row_counts, gate_blocks, gate_index, up_blocks, up_index, down_blocks, down_index):
    per_shard = NBF // N_MP

    def one_block(row_block):
        running = jnp.zeros((row_block.shape[0], D), jnp.float32)
        for shard_id in range(N_MP):
            low_block = shard_id * per_shard
            high_block = low_block + per_shard
            hidden = make_hidden(row_block, gate_blocks[low_block:high_block], gate_index[low_block:high_block],
                                 up_blocks[low_block:high_block], up_index[low_block:high_block])
            partial_sum = apply_down(hidden, down_blocks[low_block:high_block], down_index[low_block:high_block]).astype(jnp.bfloat16)
            running = running + lax.optimization_barrier(partial_sum).astype(jnp.float32)
        return running

    row_ids = jnp.arange(ROWS, dtype=jnp.int32)
    device_of = row_ids // ROWS_IN
    row_limit = jnp.take(row_counts.reshape(-1), device_of)
    valid_mask = (row_ids % ROWS_IN) < row_limit
    valid_total = BAL * N_DP * N_MP
    valid_ids = jnp.nonzero(valid_mask, size=valid_total)[0].astype(jnp.int32)
    compact = jnp.take(tokens, valid_ids, axis=0)
    block_rows = 256
    results = lax.map(one_block, compact.reshape(valid_total // block_rows, block_rows, D)).reshape(valid_total, D)
    layer_out = jnp.zeros((ROWS, D), jnp.float32).at[valid_ids].set(results)
    return layer_out.astype(jnp.bfloat16)
```

```python
import functools

import jax
import jax.numpy as jnp
from jax import lax
from jax.experimental import pallas as pl
from jax.experimental.pallas import tpu as pltpu
from jax.sharding import PartitionSpec as P

MESH = pl.DeviceIdType.MESH
CHUNKS = 4


def kernel(
    ndp, n, sl,
    tok, cnt, gate_h, gi, up_h, ui, down_h, inv,
    out,
    gate, up, down, sendp, recvp, mine, sib, xs, hid, part, sibout, sibin, rsin, rsout, yexp, back,
    w_sem, x_s, x_r, ag_s, ag_r, sb_s, sb_r, ps_s, ps_r, rs_s, rs_r, bk_s, bk_r,
):
    f32, bf16 = jnp.float32, jnp.bfloat16
    rows_in, width = tok.shape
    bal = mine.shape[1]
    nj, knz = gi.shape
    bf = gate.shape[2]
    bd = down.shape[2]
    nblk = inv.shape[1]
    ndown = down.shape[0] - 1
    chunk = width // CHUNKS
    per_slab = rows_in // ndp
    d, m = lax.axis_index("dp"), lax.axis_index("mp")
    z, c = lax.div(m, 2), lax.rem(m, 2)
    twin = 2 * z + 1 - c

    def cols_of(q):
        return pl.ds(pl.multiple_of(q * chunk, chunk), chunk)

    def slab(s):
        return pl.ds(pl.multiple_of(s * sl, sl), sl)

    def loop(count, fn):
        def step(i, carry):
            fn(i)
            return carry
        lax.fori_loop(0, count, step, 0)

    def remote(src, dst, ssem, rsem, **where):
        return pltpu.make_async_remote_copy(
            src_ref=src, dst_ref=dst, send_sem=ssem, recv_sem=rsem, device_id=where, device_id_type=MESH
        )

    loads = [
        pltpu.make_async_copy(gate_h, gate, w_sem.at[0]),
        pltpu.make_async_copy(up_h, up, w_sem.at[1]),
        pltpu.make_async_copy(down_h, down.at[pl.ds(0, ndown)], w_sem.at[2]),
    ]

    barrier = pltpu.get_barrier_semaphore()
    for s in range(1, ndp):
        pl.semaphore_signal(barrier, inc=1, device_id={"dp": lax.rem(d + s, ndp)}, device_id_type=MESH)
    pl.semaphore_signal(barrier, inc=1, device_id={"mp": twin}, device_id_type=MESH)

    @pl.when(z > 0)
    def _():
        pl.semaphore_signal(barrier, inc=1, device_id={"mp": m - 2}, device_id_type=MESH)

    @pl.when(z < n - 1)
    def _():
        pl.semaphore_signal(barrier, inc=1, device_id={"mp": m + 2}, device_id_type=MESH)

    place = lax.broadcasted_iota(jnp.int32, (ndp * sl, rows_in), 0)
    slot = lax.broadcasted_iota(jnp.int32, (ndp * sl, rows_in), 1)
    inner = lax.rem(place, sl)
    perm = ((slot == inner * ndp + lax.div(place, sl)) & (inner < per_slab)).astype(f32).astype(bf16)
    place_t = lax.broadcasted_iota(jnp.int32, (rows_in, ndp * sl), 1)
    slot_t = lax.broadcasted_iota(jnp.int32, (rows_in, ndp * sl), 0)
    inner_t = lax.rem(place_t, sl)
    perm_t = ((slot_t == inner_t * ndp + lax.div(place_t, sl)) & (inner_t < per_slab)).astype(f32).astype(bf16)

    row = lax.broadcasted_iota(jnp.int32, (bal, ndp * sl), 0)
    col = lax.broadcasted_iota(jnp.int32, (bal, ndp * sl), 1)
    row_t = lax.broadcasted_iota(jnp.int32, (ndp * sl, bal), 1)
    col_t = lax.broadcasted_iota(jnp.int32, (ndp * sl, bal), 0)
    compact = jnp.zeros((bal, ndp * sl), f32)
    expand = jnp.zeros((ndp * sl, bal), f32)
    first = jnp.int32(0)
    for s in range(ndp):
        valid = lax.div(cnt[s, m], ndp)
        low, high = s * sl, s * sl + valid
        compact += ((col >= low) & (col < high) & (row == col - low + first)).astype(f32)
        expand += ((col_t >= low) & (col_t < high) & (row_t == col_t - low + first)).astype(f32)
        first = first + valid
    compact, expand = compact.astype(bf16), expand.astype(bf16)

    def exchange(src, dst, ssem, rsem, s, q):
        peer = lax.rem(d + s, ndp)
        return remote(src.at[slab(peer), cols_of(q)], dst.at[slab(d), cols_of(q)],
                      ssem.at[s - 1, q], rsem.at[s - 1, q], dp=peer)

    def arrived(src, dst, ssem, rsem, s, q):
        peer = lax.rem(d + ndp - s, ndp)
        return remote(src.at[slab(peer), cols_of(q)], dst.at[slab(peer), cols_of(q)],
                      ssem.at[s - 1, q], rsem.at[s - 1, q], dp=peer)

    def ag_copy(o, q, mp, send_slot):
        ref = mine.at[o, :, cols_of(q)]
        return remote(ref, ref, ag_s.at[send_slot, q], ag_r.at[o, q], mp=mp)

    def twin_copy(o, q):
        return remote(mine.at[o, :, cols_of(q)], sib.at[o, :, cols_of(q)], sb_s.at[o, q], sb_r.at[o, q], mp=twin)

    def part_copy(o, q):
        return remote(sibout.at[o, :, cols_of(q)], sibin.at[o, :, cols_of(q)], ps_s.at[o, q], ps_r.at[o, q], mp=twin)

    def rs_copy(t, q, mp, dst_slot):
        return remote(rsout.at[t, :, cols_of(q)], rsin.at[dst_slot, :, cols_of(q)],
                      rs_s.at[t, q], rs_r.at[dst_slot, q], mp=mp)

    at_end = (z == 0) | (z == n - 1)

    @pl.when(at_end)
    def _():
        pl.semaphore_wait(barrier, ndp + min(n - 1, 1))

    @pl.when(jnp.logical_not(at_end))
    def _():
        pl.semaphore_wait(barrier, ndp + 2)

    def send_tokens(q):
        cols = cols_of(q)
        sendp[:, cols] = jnp.dot(perm, tok[:, cols], preferred_element_type=f32).astype(bf16)
        for s in range(1, ndp):
            exchange(sendp, recvp, x_s, x_r, s, q).start()
        recvp[slab(d), cols] = sendp[slab(d), cols]
    loop(CHUNKS, send_tokens)
    for load in loads:
        load.start()
    down[ndown] = jnp.zeros(down.shape[1:], bf16)

    def spread(q):
        cols = cols_of(q)
        for s in range(1, ndp):
            arrived(sendp, recvp, x_s, x_r, s, q).wait_recv()
        mine[z, :, cols] = jnp.dot(compact, recvp[:, cols], preferred_element_type=f32).astype(bf16)

        @pl.when(z < n - 1)
        def _():
            ag_copy(z, q, m + 2, z).start()

        @pl.when(z > 0)
        def _():
            ag_copy(z, q, m - 2, n).start()
        twin_copy(z, q).start()
    loop(CHUNKS, spread)
    for load in loads:
        load.wait()

    def unit(o):
        def wait_rows(q):
            twin_copy(o, q).wait_recv()
        loop(CHUNKS, wait_rows)
        for b in range(nblk):
            xs[b, :bal, :] = mine[o, :, b * bd:(b + 1) * bd]
            xs[b, bal:, :] = sib[o, :, b * bd:(b + 1) * bd]

        def column(j):
            def picked(index):
                return jnp.concatenate([xs[index[j, k]] for k in range(knz)], axis=1)
            gv = jnp.dot(picked(gi), gate[j], preferred_element_type=f32)
            uv = jnp.dot(picked(ui), up[j], preferred_element_type=f32)
            hid[j] = (gv / (1.0 + jnp.exp(-gv)) * uv).astype(bf16)
        loop(nj, column)

        def down_chunk(q):
            def pair(i):
                b = q * (nblk // CHUNKS) + 2 * i
                acc = jnp.zeros((2 * bal, 2 * bd), f32)
                for j in range(nj):
                    w = jnp.concatenate([down[inv[j, b]], down[inv[j, b + 1]]], axis=1)
                    acc += jnp.dot(hid[j], w, preferred_element_type=f32)
                cols = pl.ds(pl.multiple_of(b * bd, 2 * bd), 2 * bd)
                part[o, :, cols] = acc[:bal]
                sibout[o, :, cols] = acc[bal:].astype(bf16)
            loop(nblk // CHUNKS // 2, pair)
            part_copy(o, q).start()
        loop(CHUNKS, down_chunk)

    def hop(tau, q):
        cols = cols_of(q)

        def pass_on(t, has_more, slot_in, mp):
            part_copy(t, q).wait_recv()
            acc = part[t, :, cols] + sibin[t, :, cols].astype(f32)

            @pl.when(has_more)
            def _():
                rs_copy(t, q, twin, slot_in).wait_recv()
                rsout[t, :, cols] = (acc + rsin[slot_in, :, cols].astype(f32)).astype(bf16)

            @pl.when(jnp.logical_not(has_more))
            def _():
                rsout[t, :, cols] = acc.astype(bf16)
            rs_copy(t, q, mp, slot_in).start()

        left = 2 * (n - 1) - z - tau

        @pl.when((left >= 0) & (left < z))
        def _():
            pass_on(left, z < n - 1, left, m - 2)
        right = tau - z

        @pl.when((right > z) & (right < n))
        def _():
            pass_on(right, z > 0, n + right, m + 2)

    def phase(tau):
        def forward(q):
            for sign in (-1, 1):
                o = z + sign * tau

                @pl.when((o >= 0) & (o < n) & (tau > 0))
                def _():
                    ag_copy(o, q, twin, o).wait_recv()
                    beyond = z - sign

                    @pl.when((beyond >= 0) & (beyond < n))
                    def _():
                        ag_copy(o, q, m - 2 * sign, o).start()
                    twin_copy(o, q).start()
        loop(CHUNKS, forward)

        def side(i):
            o = z + (2 * i - 1) * tau

            @pl.when((o >= 0) & (o < n) & ((tau > 0) | (i == 0)))
            def _():
                unit(o)
        loop(2, side)
        loop(CHUNKS, lambda q: hop(tau, q))
    loop(n, phase)

    def finish(q):
        cols = cols_of(q)
        loop(n - 1, lambda i: hop(n + i, q))
        part_copy(z, q).wait_recv()
        part[z, :, cols] = part[z, :, cols] + sibin[z, :, cols].astype(f32)

        @pl.when(z < n - 1)
        def _():
            rs_copy(z, q, twin, z).wait_recv()
            part[z, :, cols] = part[z, :, cols] + rsin[z, :, cols].astype(f32)

        @pl.when(z > 0)
        def _():
            rs_copy(z, q, twin, n + z).wait_recv()
            part[z, :, cols] = part[z, :, cols] + rsin[n + z, :, cols].astype(f32)
        total = part[z, :, cols].astype(bf16)
        yexp[:, cols] = jnp.dot(expand, total, preferred_element_type=f32).astype(bf16)
        for s in range(1, ndp):
            exchange(yexp, back, bk_s, bk_r, s, q).start()
        back[slab(d), cols] = yexp[slab(d), cols]
    loop(CHUNKS, finish)

    def store(q):
        cols = cols_of(q)
        for s in range(1, ndp):
            arrived(yexp, back, bk_s, bk_r, s, q).wait_recv()
        out[:, cols] = jnp.dot(perm_t, back[:, cols], preferred_element_type=f32).astype(bf16)
    loop(CHUNKS, store)

    def drain(q):
        for s in range(1, ndp):
            exchange(sendp, recvp, x_s, x_r, s, q).wait_send()
            exchange(yexp, back, bk_s, bk_r, s, q).wait_send()

        @pl.when(z > 0)
        def _():
            ag_copy(z, q, m - 2, n).wait_send()

        def each(o):
            twin_copy(o, q).wait_send()
            part_copy(o, q).wait_send()

            @pl.when(((o <= z) & (z < n - 1)) | ((o > z) & (z > 0)))
            def _():
                ag_copy(o, q, twin, o).wait_send()

            @pl.when(o != z)
            def _():
                rs_copy(o, q, twin, o).wait_send()
        loop(n, each)
    loop(CHUNKS, drain)


def body(tokens, row_counts, gate_blocks, gate_index, up_blocks, up_index, down_blocks, down_index):
    ndp, nmp = lax.axis_size("dp"), lax.axis_size("mp")
    n = nmp // 2
    rows_in, width = tokens.shape
    nj, knz, bd, bf = gate_blocks.shape
    nblk = width // bd
    bal = rows_in // 2
    sl = -(-(rows_in // ndp) // 16) * 16
    ids = jnp.arange(nj * knz, dtype=jnp.int32).reshape(nj, knz)
    hit = down_index[:, :, None] == jnp.arange(nblk, dtype=jnp.int32)
    inv = jnp.min(jnp.where(hit, ids[:, :, None], nj * knz), axis=1)
    bf16 = jnp.bfloat16
    vm, sm, hbm = (pl.BlockSpec(memory_space=s) for s in (pltpu.VMEM, pltpu.SMEM, pl.ANY))
    dma = pltpu.SemaphoreType.DMA
    rows = n * 2 * bal
    return pl.pallas_call(
        functools.partial(kernel, ndp, n, sl),
        out_shape=jax.ShapeDtypeStruct(tokens.shape, bf16),
        in_specs=[vm, sm, hbm, sm, hbm, sm, hbm, sm],
        out_specs=vm,
        scratch_shapes=[
            pltpu.VMEM((nj, knz * bd, bf), bf16),
            pltpu.VMEM((nj, knz * bd, bf), bf16),
            pltpu.VMEM((nj * knz + 1, bf, bd), bf16),
            pltpu.VMEM((ndp * sl, width), bf16),
            pltpu.VMEM((ndp * sl, width), bf16),
            pltpu.VMEM((n, bal, width), bf16),
            pltpu.VMEM((n, bal, width), bf16),
            pltpu.VMEM((nblk, 2 * bal, bd), bf16),
            pltpu.VMEM((nj, 2 * bal, bf), bf16),
            pltpu.VMEM((n, bal, width), jnp.float32),
            pltpu.VMEM((n, bal, width), bf16),
            pltpu.VMEM((n, bal, width), bf16),
            pltpu.VMEM((2 * n, bal, width), bf16),
            pltpu.VMEM((n, bal, width), bf16),
            pltpu.VMEM((ndp * sl, width), bf16),
            pltpu.VMEM((ndp * sl, width), bf16),
            dma((3,)),
            dma((ndp - 1, CHUNKS)), dma((ndp - 1, CHUNKS)),
            dma((n + 1, CHUNKS)), dma((n, CHUNKS)),
            dma((n, CHUNKS)), dma((n, CHUNKS)),
            dma((n, CHUNKS)), dma((n, CHUNKS)),
            dma((n, CHUNKS)), dma((2 * n, CHUNKS)),
            dma((ndp - 1, CHUNKS)), dma((ndp - 1, CHUNKS)),
        ],
        compiler_params=pltpu.CompilerParams(
            collective_id=0, has_side_effects=True, vmem_limit_bytes=60 * 1024 * 1024
        ),
        cost_estimate=pl.CostEstimate(
            flops=6 * rows * nj * knz * bd * bf, bytes_accessed=6 * nj * knz * bd * bf, transcendentals=rows * nj * bf
        ),
    )(
        tokens, row_counts, gate_blocks.reshape(nj, knz * bd, bf), gate_index,
        up_blocks.reshape(nj, knz * bd, bf), up_index, down_blocks.reshape(nj * knz, bf, bd), inv,
    )


def solution(mesh):
    in_specs = (
        P(("dp", "mp"), None),
        P(),
        P("mp", None, None, None),
        P("mp", None),
        P("mp", None, None, None),
        P("mp", None),
        P("mp", None, None, None),
        P("mp", None),
    )
    out_specs = P(("dp", "mp"), None)
    return jax.shard_map(body, mesh=mesh, in_specs=in_specs, out_specs=out_specs, check_vma=False)
```

```python
import functools

import jax
import jax.numpy as jnp
from jax import lax
from jax.experimental import pallas as pl
from jax.experimental.pallas import tpu as pltpu
from jax.sharding import PartitionSpec as P

MESH = pl.DeviceIdType.MESH
CHUNKS = 4


def kernel(
    ndp, n, sl,
    tok, cnt, gate_h, gi, up_h, ui, down_h, inv,
    out,
    gate, up, down, sendp, recvp, mine, sib, xs, hid, prod, total, part, sibout, sibin, rsin, rsout, yexp, back,
    w_sem, x_s, x_r, ag_s, ag_r, sb_s, sb_r, ps_s, ps_r, rs_s, rs_r, bk_s, bk_r,
):
    f32, bf16 = jnp.float32, jnp.bfloat16
    rows_in, width = tok.shape
    bal = mine.shape[1]
    nj, knz = gi.shape
    bf = gate.shape[2]
    bd = down.shape[2]
    nblk = inv.shape[1]
    ndown = down.shape[0]
    chunk = width // CHUNKS
    per_slab = rows_in // ndp
    d, m = lax.axis_index("dp"), lax.axis_index("mp")
    z, c = lax.div(m, 2), lax.rem(m, 2)
    twin = 2 * z + 1 - c

    def cols_of(q):
        return pl.ds(pl.multiple_of(q * chunk, chunk), chunk)

    def slab(s):
        return pl.ds(pl.multiple_of(s * sl, sl), sl)

    def loop(count, fn):
        def step(i, carry):
            fn(i)
            return carry
        lax.fori_loop(0, count, step, 0)

    def remote(src, dst, ssem, rsem, **where):
        return pltpu.make_async_remote_copy(
            src_ref=src, dst_ref=dst, send_sem=ssem, recv_sem=rsem, device_id=where, device_id_type=MESH
        )

    loads = [
        pltpu.make_async_copy(gate_h, gate, w_sem.at[0]),
        pltpu.make_async_copy(up_h, up, w_sem.at[1]),
        pltpu.make_async_copy(down_h, down, w_sem.at[2]),
    ]

    barrier = pltpu.get_barrier_semaphore()
    for s in range(1, ndp):
        pl.semaphore_signal(barrier, inc=1, device_id={"dp": lax.rem(d + s, ndp)}, device_id_type=MESH)
    pl.semaphore_signal(barrier, inc=1, device_id={"mp": twin}, device_id_type=MESH)

    @pl.when(z > 0)
    def _():
        pl.semaphore_signal(barrier, inc=1, device_id={"mp": m - 2}, device_id_type=MESH)

    @pl.when(z < n - 1)
    def _():
        pl.semaphore_signal(barrier, inc=1, device_id={"mp": m + 2}, device_id_type=MESH)

    place = lax.broadcasted_iota(jnp.int32, (ndp * sl, rows_in), 0)
    slot = lax.broadcasted_iota(jnp.int32, (ndp * sl, rows_in), 1)
    inner = lax.rem(place, sl)
    perm = ((slot == inner * ndp + lax.div(place, sl)) & (inner < per_slab)).astype(f32).astype(bf16)
    place_t = lax.broadcasted_iota(jnp.int32, (rows_in, ndp * sl), 1)
    slot_t = lax.broadcasted_iota(jnp.int32, (rows_in, ndp * sl), 0)
    inner_t = lax.rem(place_t, sl)
    perm_t = ((slot_t == inner_t * ndp + lax.div(place_t, sl)) & (inner_t < per_slab)).astype(f32).astype(bf16)

    row = lax.broadcasted_iota(jnp.int32, (bal, ndp * sl), 0)
    col = lax.broadcasted_iota(jnp.int32, (bal, ndp * sl), 1)
    row_t = lax.broadcasted_iota(jnp.int32, (ndp * sl, bal), 1)
    col_t = lax.broadcasted_iota(jnp.int32, (ndp * sl, bal), 0)
    compact = jnp.zeros((bal, ndp * sl), f32)
    expand = jnp.zeros((ndp * sl, bal), f32)
    first = jnp.int32(0)
    for s in range(ndp):
        valid = lax.div(cnt[s, m], ndp)
        low, high = s * sl, s * sl + valid
        compact += ((col >= low) & (col < high) & (row == col - low + first)).astype(f32)
        expand += ((col_t >= low) & (col_t < high) & (row_t == col_t - low + first)).astype(f32)
        first = first + valid
    compact, expand = compact.astype(bf16), expand.astype(bf16)

    def exchange(src, dst, ssem, rsem, s, q):
        peer = lax.rem(d + s, ndp)
        return remote(src.at[slab(peer), cols_of(q)], dst.at[slab(d), cols_of(q)],
                      ssem.at[s - 1, q], rsem.at[s - 1, q], dp=peer)

    def arrived(src, dst, ssem, rsem, s, q):
        peer = lax.rem(d + ndp - s, ndp)
        return remote(src.at[slab(peer), cols_of(q)], dst.at[slab(peer), cols_of(q)],
                      ssem.at[s - 1, q], rsem.at[s - 1, q], dp=peer)

    def ag_copy(o, q, mp, send_slot):
        ref = mine.at[o, :, cols_of(q)]
        return remote(ref, ref, ag_s.at[send_slot, q], ag_r.at[o, q], mp=mp)

    def twin_copy(o, q):
        return remote(mine.at[o, :, cols_of(q)], sib.at[o, :, cols_of(q)], sb_s.at[o, q], sb_r.at[o, q], mp=twin)

    def part_copy(o, q):
        return remote(sibout.at[o, :, cols_of(q)], sibin.at[o, :, cols_of(q)], ps_s.at[o, q], ps_r.at[o, q], mp=twin)

    def rs_copy(t, q, mp, dst_slot):
        return remote(rsout.at[t, :, cols_of(q)], rsin.at[dst_slot, :, cols_of(q)],
                      rs_s.at[t, q], rs_r.at[dst_slot, q], mp=mp)

    at_end = (z == 0) | (z == n - 1)

    @pl.when(at_end)
    def _():
        pl.semaphore_wait(barrier, ndp + min(n - 1, 1))

    @pl.when(jnp.logical_not(at_end))
    def _():
        pl.semaphore_wait(barrier, ndp + 2)

    def send_tokens(q):
        cols = cols_of(q)
        sendp[:, cols] = jnp.dot(perm, tok[:, cols], preferred_element_type=f32).astype(bf16)
        for s in range(1, ndp):
            exchange(sendp, recvp, x_s, x_r, s, q).start()
        recvp[slab(d), cols] = sendp[slab(d), cols]
    loop(CHUNKS, send_tokens)
    for load in loads:
        load.start()
    prod[ndown] = jnp.zeros(prod.shape[1:], f32)

    def spread(q):
        cols = cols_of(q)
        for s in range(1, ndp):
            arrived(sendp, recvp, x_s, x_r, s, q).wait_recv()
        mine[z, :, cols] = jnp.dot(compact, recvp[:, cols], preferred_element_type=f32).astype(bf16)

        @pl.when(z < n - 1)
        def _():
            ag_copy(z, q, m + 2, z).start()

        @pl.when(z > 0)
        def _():
            ag_copy(z, q, m - 2, n).start()
        twin_copy(z, q).start()
    loop(CHUNKS, spread)
    for load in loads:
        load.wait()

    def take(o, q, sign):
        ag_copy(o, q, twin, o).wait_recv()
        beyond = z - sign

        @pl.when((beyond >= 0) & (beyond < n))
        def _():
            ag_copy(o, q, m - 2 * sign, o).start()
        twin_copy(o, q).start()

    def take_all(tau, q, passing):
        for sign in (-1, 1):
            o, beyond = z + sign * tau, z - sign
            inside = (beyond >= 0) & (beyond < n)
            wanted = inside if passing else jnp.logical_not(inside)

            @pl.when((o >= 0) & (o < n) & (tau > 0) & wanted)
            def _():
                take(o, q, sign)

    def unit(o, tau, last):
        def wait_rows(q):
            twin_copy(o, q).wait_recv()
        loop(CHUNKS, wait_rows)
        for b in range(nblk):
            xs[b, :bal, :] = mine[o, :, b * bd:(b + 1) * bd]
            xs[b, bal:, :] = sib[o, :, b * bd:(b + 1) * bd]

        group = nj // CHUNKS

        def columns(q):
            for i in range(group):
                j = q * group + i

                def picked(index):
                    return jnp.concatenate([xs[index[j, k]] for k in range(knz)], axis=1)
                gv = jnp.dot(picked(gi), gate[j], preferred_element_type=f32)
                uv = jnp.dot(picked(ui), up[j], preferred_element_type=f32)
                hid[j] = (gv / (1.0 + jnp.exp(-gv)) * uv).astype(bf16)

            @pl.when(last)
            def _():
                take_all(tau + 1, q, True)
        loop(CHUNKS, columns)

        def down_row(j):
            h = hid[j]
            for i in range(0, knz, 2):
                w = jnp.concatenate([down[j * knz + i], down[j * knz + i + 1]], axis=1)
                p = jnp.dot(h, w, preferred_element_type=f32)
                prod[j * knz + i] = p[:, :bd]
                prod[j * knz + i + 1] = p[:, bd:]
        loop(nj, down_row)

        def gather(q):
            def some(i):
                for e in range(4):
                    b = q * (nblk // CHUNKS) + 4 * i + e
                    acc = prod[inv[0, b]]
                    for j in range(1, nj):
                        acc += prod[inv[j, b]]
                    cols = pl.ds(pl.multiple_of(b * bd, bd), bd)
                    part[o, :, cols] = acc[:bal].astype(bf16)
                    sibout[o, :, cols] = acc[bal:].astype(bf16)
            loop(nblk // CHUNKS // 4, some)
            part_copy(o, q).start()
        loop(CHUNKS, gather)

    def hop(tau, q):
        cols = cols_of(q)

        def pass_on(t, has_more, slot_in, mp):
            part_copy(t, q).wait_recv()
            acc = part[t, :, cols].astype(f32) + sibin[t, :, cols].astype(f32)

            @pl.when(has_more)
            def _():
                rs_copy(t, q, twin, slot_in).wait_recv()
                rsout[t, :, cols] = (acc + rsin[slot_in, :, cols].astype(f32)).astype(bf16)

            @pl.when(jnp.logical_not(has_more))
            def _():
                rsout[t, :, cols] = acc.astype(bf16)
            rs_copy(t, q, mp, slot_in).start()

        left = 2 * (n - 1) - z - tau

        @pl.when((left >= 0) & (left < z))
        def _():
            pass_on(left, z < n - 1, left, m - 2)
        right = tau - z

        @pl.when((right > z) & (right < n))
        def _():
            pass_on(right, z > 0, n + right, m + 2)

    def phase(tau):
        loop(CHUNKS, lambda q: take_all(tau, q, False))

        def side(i):
            o = z + (2 * i - 1) * tau

            @pl.when((o >= 0) & (o < n) & ((tau > 0) | (i == 0)))
            def _():
                unit(o, tau, (i == 1) | (tau == 0) | (z + tau >= n))
        loop(2, side)
        loop(CHUNKS, lambda q: hop(tau, q))
    loop(n, phase)

    def finish(q):
        cols = cols_of(q)
        loop(n - 1, lambda i: hop(n + i, q))
        part_copy(z, q).wait_recv()
        total[...] = part[z, :, cols].astype(f32) + sibin[z, :, cols].astype(f32)

        @pl.when(z < n - 1)
        def _():
            rs_copy(z, q, twin, z).wait_recv()
            total[...] += rsin[z, :, cols].astype(f32)

        @pl.when(z > 0)
        def _():
            rs_copy(z, q, twin, n + z).wait_recv()
            total[...] += rsin[n + z, :, cols].astype(f32)
        yexp[:, cols] = jnp.dot(expand, total[...].astype(bf16), preferred_element_type=f32).astype(bf16)
        for s in range(1, ndp):
            exchange(yexp, back, bk_s, bk_r, s, q).start()
        back[slab(d), cols] = yexp[slab(d), cols]
    loop(CHUNKS, finish)

    def store(q):
        cols = cols_of(q)
        for s in range(1, ndp):
            arrived(yexp, back, bk_s, bk_r, s, q).wait_recv()
        out[:, cols] = jnp.dot(perm_t, back[:, cols], preferred_element_type=f32).astype(bf16)
    loop(CHUNKS, store)

    def drain(q):
        for s in range(1, ndp):
            exchange(sendp, recvp, x_s, x_r, s, q).wait_send()
            exchange(yexp, back, bk_s, bk_r, s, q).wait_send()

        @pl.when(z > 0)
        def _():
            ag_copy(z, q, m - 2, n).wait_send()

        def each(o):
            twin_copy(o, q).wait_send()
            part_copy(o, q).wait_send()

            @pl.when(((o <= z) & (z < n - 1)) | ((o > z) & (z > 0)))
            def _():
                ag_copy(o, q, twin, o).wait_send()

            @pl.when(o != z)
            def _():
                rs_copy(o, q, twin, o).wait_send()
        loop(n, each)
    loop(CHUNKS, drain)


def body(tokens, row_counts, gate_blocks, gate_index, up_blocks, up_index, down_blocks, down_index):
    ndp, nmp = lax.axis_size("dp"), lax.axis_size("mp")
    n = nmp // 2
    rows_in, width = tokens.shape
    nj, knz, bd, bf = gate_blocks.shape
    nblk = width // bd
    bal = rows_in // 2
    sl = -(-(rows_in // ndp) // 16) * 16
    ids = jnp.arange(nj * knz, dtype=jnp.int32).reshape(nj, knz)
    hit = down_index[:, :, None] == jnp.arange(nblk, dtype=jnp.int32)
    inv = jnp.min(jnp.where(hit, ids[:, :, None], nj * knz), axis=1)
    bf16 = jnp.bfloat16
    vm, sm, hbm = (pl.BlockSpec(memory_space=s) for s in (pltpu.VMEM, pltpu.SMEM, pl.ANY))
    dma = pltpu.SemaphoreType.DMA
    rows = n * 2 * bal
    return pl.pallas_call(
        functools.partial(kernel, ndp, n, sl),
        out_shape=jax.ShapeDtypeStruct(tokens.shape, bf16),
        in_specs=[vm, sm, hbm, sm, hbm, sm, hbm, sm],
        out_specs=vm,
        scratch_shapes=[
            pltpu.VMEM((nj, knz * bd, bf), bf16),
            pltpu.VMEM((nj, knz * bd, bf), bf16),
            pltpu.VMEM((nj * knz, bf, bd), bf16),
            pltpu.VMEM((ndp * sl, width), bf16),
            pltpu.VMEM((ndp * sl, width), bf16),
            pltpu.VMEM((n, bal, width), bf16),
            pltpu.VMEM((n, bal, width), bf16),
            pltpu.VMEM((nblk, 2 * bal, bd), bf16),
            pltpu.VMEM((nj, 2 * bal, bf), bf16),
            pltpu.VMEM((nj * knz + 1, 2 * bal, bd), jnp.float32),
            pltpu.VMEM((bal, width // CHUNKS), jnp.float32),
            pltpu.VMEM((n, bal, width), bf16),
            pltpu.VMEM((n, bal, width), bf16),
            pltpu.VMEM((n, bal, width), bf16),
            pltpu.VMEM((2 * n, bal, width), bf16),
            pltpu.VMEM((n, bal, width), bf16),
            pltpu.VMEM((ndp * sl, width), bf16),
            pltpu.VMEM((ndp * sl, width), bf16),
            dma((3,)),
            dma((ndp - 1, CHUNKS)), dma((ndp - 1, CHUNKS)),
            dma((n + 1, CHUNKS)), dma((n, CHUNKS)),
            dma((n, CHUNKS)), dma((n, CHUNKS)),
            dma((n, CHUNKS)), dma((n, CHUNKS)),
            dma((n, CHUNKS)), dma((2 * n, CHUNKS)),
            dma((ndp - 1, CHUNKS)), dma((ndp - 1, CHUNKS)),
        ],
        compiler_params=pltpu.CompilerParams(
            collective_id=0, has_side_effects=True, vmem_limit_bytes=60 * 1024 * 1024
        ),
        cost_estimate=pl.CostEstimate(
            flops=6 * rows * nj * knz * bd * bf, bytes_accessed=6 * nj * knz * bd * bf, transcendentals=rows * nj * bf
        ),
    )(
        tokens, row_counts, gate_blocks.reshape(nj, knz * bd, bf), gate_index,
        up_blocks.reshape(nj, knz * bd, bf), up_index, down_blocks.reshape(nj * knz, bf, bd), inv,
    )


def solution(mesh):
    in_specs = (
        P(("dp", "mp"), None),
        P(),
        P("mp", None, None, None),
        P("mp", None),
        P("mp", None, None, None),
        P("mp", None),
        P("mp", None, None, None),
        P("mp", None),
    )
    out_specs = P(("dp", "mp"), None)
    return jax.shard_map(body, mesh=mesh, in_specs=in_specs, out_specs=out_specs, check_vma=False)
```

```python
import functools

import jax
import jax.numpy as jnp
from jax import lax
from jax.experimental import pallas as pl
from jax.experimental.pallas import tpu as pltpu
from jax.sharding import PartitionSpec as P

MESH = pl.DeviceIdType.MESH
CHUNKS = 4


def kernel(
    ndp, n, sl,
    tok, cnt, gate_h, gi, up_h, ui, down_h, inv,
    out,
    gate, up, down, sendp, recvp, mine, sib, xs, hid, prod, total, part, sibout, sibin, rsin, back,
    w_sem, x_s, x_r, ag_s, ag_r, sb_s, sb_r, ps_s, ps_r, rs_s, rs_r, bk_s, bk_r,
):
    f32, bf16 = jnp.float32, jnp.bfloat16
    rows_in, width = tok.shape
    bal = mine.shape[1]
    nj, knz = gi.shape
    bf = gate.shape[2]
    bd = down.shape[2]
    nblk = inv.shape[1]
    ndown = down.shape[0]
    chunk = width // CHUNKS
    per_slab = rows_in // ndp
    d, m = lax.axis_index("dp"), lax.axis_index("mp")
    z, c = lax.div(m, 2), lax.rem(m, 2)
    twin = 2 * z + 1 - c

    def cols_of(q):
        return pl.ds(pl.multiple_of(q * chunk, chunk), chunk)

    def slab(s):
        return pl.ds(pl.multiple_of(s * sl, sl), sl)

    def loop(count, fn):
        def step(i, carry):
            fn(i)
            return carry
        lax.fori_loop(0, count, step, 0)

    def remote(src, dst, ssem, rsem, **where):
        return pltpu.make_async_remote_copy(
            src_ref=src, dst_ref=dst, send_sem=ssem, recv_sem=rsem, device_id=where, device_id_type=MESH
        )

    loads = [
        pltpu.make_async_copy(gate_h, gate, w_sem.at[0]),
        pltpu.make_async_copy(up_h, up, w_sem.at[1]),
        pltpu.make_async_copy(down_h, down, w_sem.at[2]),
    ]

    barrier = pltpu.get_barrier_semaphore()
    for s in range(1, ndp):
        pl.semaphore_signal(barrier, inc=1, device_id={"dp": lax.rem(d + s, ndp)}, device_id_type=MESH)
    pl.semaphore_signal(barrier, inc=1, device_id={"mp": twin}, device_id_type=MESH)

    @pl.when(z > 0)
    def _():
        pl.semaphore_signal(barrier, inc=1, device_id={"mp": m - 2}, device_id_type=MESH)

    @pl.when(z < n - 1)
    def _():
        pl.semaphore_signal(barrier, inc=1, device_id={"mp": m + 2}, device_id_type=MESH)

    place = lax.broadcasted_iota(jnp.int32, (ndp * sl, rows_in), 0)
    slot = lax.broadcasted_iota(jnp.int32, (ndp * sl, rows_in), 1)
    inner = lax.rem(place, sl)
    perm = ((slot == inner * ndp + lax.div(place, sl)) & (inner < per_slab)).astype(f32).astype(bf16)
    place_t = lax.broadcasted_iota(jnp.int32, (rows_in, ndp * sl), 1)
    slot_t = lax.broadcasted_iota(jnp.int32, (rows_in, ndp * sl), 0)
    inner_t = lax.rem(place_t, sl)
    perm_t = ((slot_t == inner_t * ndp + lax.div(place_t, sl)) & (inner_t < per_slab)).astype(f32).astype(bf16)

    row = lax.broadcasted_iota(jnp.int32, (bal, ndp * sl), 0)
    col = lax.broadcasted_iota(jnp.int32, (bal, ndp * sl), 1)
    row_t = lax.broadcasted_iota(jnp.int32, (ndp * sl, bal), 1)
    col_t = lax.broadcasted_iota(jnp.int32, (ndp * sl, bal), 0)
    compact = jnp.zeros((bal, ndp * sl), f32)
    expand = jnp.zeros((ndp * sl, bal), f32)
    first = jnp.int32(0)
    for s in range(ndp):
        valid = lax.div(cnt[s, m], ndp)
        low, high = s * sl, s * sl + valid
        compact += ((col >= low) & (col < high) & (row == col - low + first)).astype(f32)
        expand += ((col_t >= low) & (col_t < high) & (row_t == col_t - low + first)).astype(f32)
        first = first + valid
    compact, expand = compact.astype(bf16), expand.astype(bf16)

    def exchange(src, dst, ssem, rsem, s, q):
        peer = lax.rem(d + s, ndp)
        return remote(src.at[slab(peer), cols_of(q)], dst.at[slab(d), cols_of(q)],
                      ssem.at[s - 1, q], rsem.at[s - 1, q], dp=peer)

    def arrived(src, dst, ssem, rsem, s, q):
        peer = lax.rem(d + ndp - s, ndp)
        return remote(src.at[slab(peer), cols_of(q)], dst.at[slab(peer), cols_of(q)],
                      ssem.at[s - 1, q], rsem.at[s - 1, q], dp=peer)

    def ag_copy(o, q, mp, send_slot):
        ref = mine.at[o, :, cols_of(q)]
        return remote(ref, ref, ag_s.at[send_slot, q], ag_r.at[o, q], mp=mp)

    def twin_copy(o, q):
        return remote(mine.at[o, :, cols_of(q)], sib.at[o, :, cols_of(q)], sb_s.at[o, q], sb_r.at[o, q], mp=twin)

    def part_copy(o, q):
        return remote(sibout.at[o, :, cols_of(q)], sibin.at[o, :, cols_of(q)], ps_s.at[o, q], ps_r.at[o, q], mp=twin)

    def rs_copy(t, q, mp, dst_slot):
        return remote(part.at[t, :, cols_of(q)], rsin.at[dst_slot, :, cols_of(q)],
                      rs_s.at[t, q], rs_r.at[dst_slot, q], mp=mp)

    at_end = (z == 0) | (z == n - 1)

    @pl.when(at_end)
    def _():
        pl.semaphore_wait(barrier, ndp + min(n - 1, 1))

    @pl.when(jnp.logical_not(at_end))
    def _():
        pl.semaphore_wait(barrier, ndp + 2)

    def send_tokens(q):
        cols = cols_of(q)
        sendp[:, cols] = jnp.dot(perm, tok[:, cols], preferred_element_type=f32).astype(bf16)
        for s in range(1, ndp):
            exchange(sendp, recvp, x_s, x_r, s, q).start()
        recvp[slab(d), cols] = sendp[slab(d), cols]
    loop(CHUNKS, send_tokens)
    for load in loads:
        load.start()
    prod[ndown] = jnp.zeros(prod.shape[1:], bf16)

    def take(o, q, sign):
        ag_copy(o, q, twin, o).wait_recv()
        beyond = z - sign

        @pl.when((beyond >= 0) & (beyond < n))
        def _():
            ag_copy(o, q, m - 2 * sign, o).start()
        twin_copy(o, q).start()

    def take_all(tau, q, passing):
        for sign in (-1, 1):
            o, beyond = z + sign * tau, z - sign
            inside = (beyond >= 0) & (beyond < n)
            wanted = inside if passing else jnp.logical_not(inside)

            @pl.when((o >= 0) & (o < n) & wanted)
            def _():
                take(o, q, sign)

    def spread(q):
        cols = cols_of(q)
        for s in range(1, ndp):
            arrived(sendp, recvp, x_s, x_r, s, q).wait_recv()
        mine[z, :, cols] = jnp.dot(compact, recvp[:, cols], preferred_element_type=f32).astype(bf16)

        @pl.when(z < n - 1)
        def _():
            ag_copy(z, q, m + 2, z).start()

        @pl.when(z > 0)
        def _():
            ag_copy(z, q, m - 2, n).start()
        twin_copy(z, q).start()

        @pl.when(q > 0)
        def _():
            take_all(1, q - 1, True)
            take_all(1, q - 1, False)
    loop(CHUNKS, spread)
    take_all(1, CHUNKS - 1, True)
    take_all(1, CHUNKS - 1, False)
    for load in loads:
        load.wait()

    def unit(origins, tau, last):
        rows = pl.ds(0, 2 * bal * len(origins))

        def wait_rows(q):
            for o in origins:
                twin_copy(o, q).wait_recv()
        loop(CHUNKS, wait_rows)
        for i, o in enumerate(origins):
            top = 2 * bal * i
            for b in range(nblk):
                xs[b, top:top + bal, :] = mine[o, :, b * bd:(b + 1) * bd]
                xs[b, top + bal:top + 2 * bal, :] = sib[o, :, b * bd:(b + 1) * bd]

        steps = min(nj, CHUNKS)
        group, passes = nj // steps, CHUNKS // steps

        def columns(g):
            for i in range(group):
                j = g * group + i

                def picked(index):
                    return jnp.concatenate([xs[index[j, k], rows, :] for k in range(knz)], axis=1)
                gv = jnp.dot(picked(gi), gate[j], preferred_element_type=f32)
                uv = jnp.dot(picked(ui), up[j], preferred_element_type=f32)
                hid[j, rows, :] = (gv / (1.0 + jnp.exp(-gv)) * uv).astype(bf16)
            if last is not None:
                @pl.when(last)
                def _():
                    for i in range(passes):
                        take_all(tau + 1, g * passes + i, True)
        loop(steps, columns)

        def down_row(j):
            h = hid[j, rows, :]
            for i in range(0, knz, 4):
                w = jnp.concatenate([down[j * knz + i + e] for e in range(4)], axis=1)
                p = jnp.dot(h, w, preferred_element_type=f32).astype(bf16)
                for e in range(4):
                    prod[j * knz + i + e, rows, :] = p[:, e * bd:(e + 1) * bd]
        loop(nj, down_row)

        def gather(q):
            def some(i):
                for e in range(2):
                    b = q * (nblk // CHUNKS) + 2 * i + e
                    acc = prod[inv[0, b], rows, :].astype(f32)
                    for j in range(1, nj):
                        acc += prod[inv[j, b], rows, :].astype(f32)
                    cols = pl.ds(pl.multiple_of(b * bd, bd), bd)
                    acc = acc.astype(bf16)
                    for r, o in enumerate(origins):
                        top = 2 * bal * r
                        part[o, :, cols] = acc[top:top + bal]
                        sibout[o, :, cols] = acc[top + bal:top + 2 * bal]
            loop(nblk // CHUNKS // 2, some)
            for o in origins:
                part_copy(o, q).start()
        loop(CHUNKS, gather)

    def hop(tau, q):
        cols = cols_of(q)

        def pass_on(t, has_more, slot_in, mp):
            part_copy(t, q).wait_recv()
            acc = part[t, :, cols].astype(f32) + sibin[t, :, cols].astype(f32)

            @pl.when(has_more)
            def _():
                rs_copy(t, q, twin, slot_in).wait_recv()
                part[t, :, cols] = (acc + rsin[slot_in, :, cols].astype(f32)).astype(bf16)

            @pl.when(jnp.logical_not(has_more))
            def _():
                part[t, :, cols] = acc.astype(bf16)
            rs_copy(t, q, mp, slot_in).start()

        left = 2 * (n - 1) - z - tau

        @pl.when((left >= 0) & (left < z))
        def _():
            pass_on(left, z < n - 1, left, m - 2)
        right = tau - z

        @pl.when((right > z) & (right < n))
        def _():
            pass_on(right, z > 0, n + right, m + 2)

    def near(i):
        o = z + 2 * i - 1

        @pl.when(at_end & (o >= 0) & (o < n))
        def _():
            unit([z, o], 1, None)
    loop(2, near)
    if n > 2:
        @pl.when(jnp.logical_not(at_end))
        def _():
            unit([z, z - 1, z + 1], 1, z >= 0)
    loop(CHUNKS, lambda q: hop(1, q))

    def phase(i):
        tau = i + 2
        loop(CHUNKS, lambda q: take_all(tau, q, False))

        def side(i):
            o = z + (2 * i - 1) * tau

            @pl.when((o >= 0) & (o < n))
            def _():
                unit([o], tau, (i == 1) | (z + tau >= n))
        loop(2, side)
        loop(CHUNKS, lambda q: hop(tau, q))
    loop(n - 2, phase)

    def finish(q):
        cols = cols_of(q)
        for s in range(1, ndp):
            exchange(sendp, recvp, x_s, x_r, s, q).wait_send()
        loop(n - 1, lambda i: hop(n + i, q))
        part_copy(z, q).wait_recv()
        total[...] = part[z, :, cols].astype(f32) + sibin[z, :, cols].astype(f32)

        @pl.when(z < n - 1)
        def _():
            rs_copy(z, q, twin, z).wait_recv()
            total[...] += rsin[z, :, cols].astype(f32)

        @pl.when(z > 0)
        def _():
            rs_copy(z, q, twin, n + z).wait_recv()
            total[...] += rsin[n + z, :, cols].astype(f32)
        sendp[:, cols] = jnp.dot(expand, total[...].astype(bf16), preferred_element_type=f32).astype(bf16)
        for s in range(1, ndp):
            exchange(sendp, back, bk_s, bk_r, s, q).start()
        back[slab(d), cols] = sendp[slab(d), cols]
    loop(CHUNKS, finish)

    def store(q):
        cols = cols_of(q)
        for s in range(1, ndp):
            arrived(sendp, back, bk_s, bk_r, s, q).wait_recv()
        out[:, cols] = jnp.dot(perm_t, back[:, cols], preferred_element_type=f32).astype(bf16)
    loop(CHUNKS, store)

    def drain(q):
        for s in range(1, ndp):
            exchange(sendp, back, bk_s, bk_r, s, q).wait_send()

        @pl.when(z > 0)
        def _():
            ag_copy(z, q, m - 2, n).wait_send()

        def each(o):
            twin_copy(o, q).wait_send()
            part_copy(o, q).wait_send()

            @pl.when(((o <= z) & (z < n - 1)) | ((o > z) & (z > 0)))
            def _():
                ag_copy(o, q, twin, o).wait_send()

            @pl.when(o != z)
            def _():
                rs_copy(o, q, twin, o).wait_send()
        loop(n, each)
    loop(CHUNKS, drain)


def body(tokens, row_counts, gate_blocks, gate_index, up_blocks, up_index, down_blocks, down_index):
    ndp, nmp = lax.axis_size("dp"), lax.axis_size("mp")
    n = nmp // 2
    rows_in, width = tokens.shape
    nj, knz, bd, bf = gate_blocks.shape
    nblk = width // bd
    bal = rows_in // 2
    sl = -(-(rows_in // ndp) // 16) * 16
    ids = jnp.arange(nj * knz, dtype=jnp.int32).reshape(nj, knz)
    hit = down_index[:, :, None] == jnp.arange(nblk, dtype=jnp.int32)
    inv = jnp.min(jnp.where(hit, ids[:, :, None], nj * knz), axis=1)
    bf16 = jnp.bfloat16
    vm, sm, hbm = (pl.BlockSpec(memory_space=s) for s in (pltpu.VMEM, pltpu.SMEM, pl.ANY))
    dma = pltpu.SemaphoreType.DMA
    rows = n * 2 * bal
    tall = 2 * bal * min(n, 3)
    return pl.pallas_call(
        functools.partial(kernel, ndp, n, sl),
        out_shape=jax.ShapeDtypeStruct(tokens.shape, bf16),
        in_specs=[vm, sm, hbm, sm, hbm, sm, hbm, sm],
        out_specs=vm,
        scratch_shapes=[
            pltpu.VMEM((nj, knz * bd, bf), bf16),
            pltpu.VMEM((nj, knz * bd, bf), bf16),
            pltpu.VMEM((nj * knz, bf, bd), bf16),
            pltpu.VMEM((ndp * sl, width), bf16),
            pltpu.VMEM((ndp * sl, width), bf16),
            pltpu.VMEM((n, bal, width), bf16),
            pltpu.VMEM((n, bal, width), bf16),
            pltpu.VMEM((nblk, tall, bd), bf16),
            pltpu.VMEM((nj, tall, bf), bf16),
            pltpu.VMEM((nj * knz + 1, tall, bd), bf16),
            pltpu.VMEM((bal, width // CHUNKS), jnp.float32),
            pltpu.VMEM((n, bal, width), bf16),
            pltpu.VMEM((n, bal, width), bf16),
            pltpu.VMEM((n, bal, width), bf16),
            pltpu.VMEM((2 * n, bal, width), bf16),
            pltpu.VMEM((ndp * sl, width), bf16),
            dma((3,)),
            dma((ndp - 1, CHUNKS)), dma((ndp - 1, CHUNKS)),
            dma((n + 1, CHUNKS)), dma((n, CHUNKS)),
            dma((n, CHUNKS)), dma((n, CHUNKS)),
            dma((n, CHUNKS)), dma((n, CHUNKS)),
            dma((n, CHUNKS)), dma((2 * n, CHUNKS)),
            dma((ndp - 1, CHUNKS)), dma((ndp - 1, CHUNKS)),
        ],
        compiler_params=pltpu.CompilerParams(
            collective_id=0, has_side_effects=True, vmem_limit_bytes=60 * 1024 * 1024
        ),
        cost_estimate=pl.CostEstimate(
            flops=6 * rows * nj * knz * bd * bf, bytes_accessed=6 * nj * knz * bd * bf, transcendentals=rows * nj * bf
        ),
    )(
        tokens, row_counts, gate_blocks.reshape(nj, knz * bd, bf), gate_index,
        up_blocks.reshape(nj, knz * bd, bf), up_index, down_blocks.reshape(nj * knz, bf, bd), inv,
    )


def solution(mesh):
    in_specs = (
        P(("dp", "mp"), None),
        P(),
        P("mp", None, None, None),
        P("mp", None),
        P("mp", None, None, None),
        P("mp", None),
        P("mp", None, None, None),
        P("mp", None),
    )
    out_specs = P(("dp", "mp"), None)
    return jax.shard_map(body, mesh=mesh, in_specs=in_specs, out_specs=out_specs, check_vma=False)
```

```python
import functools

import jax
import jax.numpy as jnp
from jax import lax
from jax.experimental import pallas as pl
from jax.experimental.pallas import tpu as pltpu
from jax.sharding import PartitionSpec as P

MESH = pl.DeviceIdType.MESH
CHUNKS = 8


def kernel(
    ndp, n, sl,
    tok, cnt, gate_h, gi, up_h, ui, down_h, inv,
    out,
    gate, up, down, sendp, recvp, mine, sib, xs, hid, prod, total, part, sibout, sibin, rsin, back,
    w_sem, x_s, x_r, ag_s, ag_r, sb_s, sb_r, ps_s, ps_r, rs_s, rs_r, bk_s, bk_r,
):
    f32, bf16 = jnp.float32, jnp.bfloat16
    rows_in, width = tok.shape
    bal = mine.shape[1]
    nj, knz = gi.shape
    bf = gate.shape[2]
    bd = down.shape[2]
    nblk = inv.shape[1]
    ndown = down.shape[0]
    chunk = width // CHUNKS
    per_slab = rows_in // ndp
    d, m = lax.axis_index("dp"), lax.axis_index("mp")
    z, c = lax.div(m, 2), lax.rem(m, 2)
    twin = 2 * z + 1 - c

    def cols_of(q):
        return pl.ds(pl.multiple_of(q * chunk, chunk), chunk)

    def slab(s):
        return pl.ds(pl.multiple_of(s * sl, sl), sl)

    def loop(count, fn):
        def step(i, carry):
            fn(i)
            return carry
        lax.fori_loop(0, count, step, 0)

    def remote(src, dst, ssem, rsem, **where):
        return pltpu.make_async_remote_copy(
            src_ref=src, dst_ref=dst, send_sem=ssem, recv_sem=rsem, device_id=where, device_id_type=MESH
        )

    loads = [
        pltpu.make_async_copy(gate_h, gate, w_sem.at[0]),
        pltpu.make_async_copy(up_h, up, w_sem.at[1]),
        pltpu.make_async_copy(down_h, down, w_sem.at[2]),
    ]

    barrier = pltpu.get_barrier_semaphore()
    for s in range(1, ndp):
        pl.semaphore_signal(barrier, inc=1, device_id={"dp": lax.rem(d + s, ndp)}, device_id_type=MESH)
    pl.semaphore_signal(barrier, inc=1, device_id={"mp": twin}, device_id_type=MESH)

    @pl.when(z > 0)
    def _():
        pl.semaphore_signal(barrier, inc=1, device_id={"mp": m - 2}, device_id_type=MESH)

    @pl.when(z < n - 1)
    def _():
        pl.semaphore_signal(barrier, inc=1, device_id={"mp": m + 2}, device_id_type=MESH)

    place = lax.broadcasted_iota(jnp.int32, (ndp * sl, rows_in), 0)
    slot = lax.broadcasted_iota(jnp.int32, (ndp * sl, rows_in), 1)
    inner = lax.rem(place, sl)
    perm = ((slot == inner * ndp + lax.div(place, sl)) & (inner < per_slab)).astype(f32).astype(bf16)
    place_t = lax.broadcasted_iota(jnp.int32, (rows_in, ndp * sl), 1)
    slot_t = lax.broadcasted_iota(jnp.int32, (rows_in, ndp * sl), 0)
    inner_t = lax.rem(place_t, sl)
    perm_t = ((slot_t == inner_t * ndp + lax.div(place_t, sl)) & (inner_t < per_slab)).astype(f32).astype(bf16)

    row = lax.broadcasted_iota(jnp.int32, (bal, ndp * sl), 0)
    col = lax.broadcasted_iota(jnp.int32, (bal, ndp * sl), 1)
    row_t = lax.broadcasted_iota(jnp.int32, (ndp * sl, bal), 1)
    col_t = lax.broadcasted_iota(jnp.int32, (ndp * sl, bal), 0)
    compact = jnp.zeros((bal, ndp * sl), f32)
    expand = jnp.zeros((ndp * sl, bal), f32)
    first = jnp.int32(0)
    for s in range(ndp):
        valid = lax.div(cnt[s, m], ndp)
        low, high = s * sl, s * sl + valid
        compact += ((col >= low) & (col < high) & (row == col - low + first)).astype(f32)
        expand += ((col_t >= low) & (col_t < high) & (row_t == col_t - low + first)).astype(f32)
        first = first + valid
    compact, expand = compact.astype(bf16), expand.astype(bf16)

    def exchange(src, dst, ssem, rsem, s, q):
        peer = lax.rem(d + s, ndp)
        return remote(src.at[slab(peer), cols_of(q)], dst.at[slab(d), cols_of(q)],
                      ssem.at[s - 1, q], rsem.at[s - 1, q], dp=peer)

    def arrived(src, dst, ssem, rsem, s, q):
        peer = lax.rem(d + ndp - s, ndp)
        return remote(src.at[slab(peer), cols_of(q)], dst.at[slab(peer), cols_of(q)],
                      ssem.at[s - 1, q], rsem.at[s - 1, q], dp=peer)

    def ag_copy(o, q, mp, send_slot):
        ref = mine.at[o, :, cols_of(q)]
        return remote(ref, ref, ag_s.at[send_slot, q], ag_r.at[o, q], mp=mp)

    def twin_copy(o, q):
        return remote(mine.at[o, :, cols_of(q)], sib.at[o, :, cols_of(q)], sb_s.at[o, q], sb_r.at[o, q], mp=twin)

    def part_copy(o, q):
        return remote(sibout.at[o, :, cols_of(q)], sibin.at[o, :, cols_of(q)], ps_s.at[o, q], ps_r.at[o, q], mp=twin)

    def rs_copy(t, q, mp, dst_slot):
        return remote(part.at[t, :, cols_of(q)], rsin.at[dst_slot, :, cols_of(q)],
                      rs_s.at[t, q], rs_r.at[dst_slot, q], mp=mp)

    at_end = (z == 0) | (z == n - 1)

    @pl.when(at_end)
    def _():
        pl.semaphore_wait(barrier, ndp + min(n - 1, 1))

    @pl.when(jnp.logical_not(at_end))
    def _():
        pl.semaphore_wait(barrier, ndp + 2)

    def send_tokens(q):
        cols = cols_of(q)
        sendp[:, cols] = jnp.dot(perm, tok[:, cols], preferred_element_type=f32).astype(bf16)
        for s in range(1, ndp):
            exchange(sendp, recvp, x_s, x_r, s, q).start()
        recvp[slab(d), cols] = sendp[slab(d), cols]
    loop(CHUNKS, send_tokens)
    for load in loads:
        load.start()
    prod[ndown] = jnp.zeros(prod.shape[1:], f32)

    def take(o, q, sign):
        ag_copy(o, q, twin, o).wait_recv()
        beyond = z - sign

        @pl.when((beyond >= 0) & (beyond < n))
        def _():
            ag_copy(o, q, m - 2 * sign, o).start()
        twin_copy(o, q).start()

    def take_all(tau, q, passing):
        for sign in (-1, 1):
            o, beyond = z + sign * tau, z - sign
            inside = (beyond >= 0) & (beyond < n)
            wanted = inside if passing else jnp.logical_not(inside)

            @pl.when((o >= 0) & (o < n) & wanted)
            def _():
                take(o, q, sign)

    def spread(q):
        cols = cols_of(q)
        for s in range(1, ndp):
            arrived(sendp, recvp, x_s, x_r, s, q).wait_recv()
        mine[z, :, cols] = jnp.dot(compact, recvp[:, cols], preferred_element_type=f32).astype(bf16)

        @pl.when(z < n - 1)
        def _():
            ag_copy(z, q, m + 2, z).start()

        @pl.when(z > 0)
        def _():
            ag_copy(z, q, m - 2, n).start()
        twin_copy(z, q).start()

        @pl.when(q > 0)
        def _():
            take_all(1, q - 1, True)
            take_all(1, q - 1, False)
    loop(CHUNKS, spread)
    take_all(1, CHUNKS - 1, True)
    take_all(1, CHUNKS - 1, False)
    for load in loads:
        load.wait()

    def hop(tau, q):
        cols = cols_of(q)

        def pass_on(t, has_more, slot_in, mp):
            part_copy(t, q).wait_recv()
            acc = part[t, :, cols].astype(f32) + sibin[t, :, cols].astype(f32)

            @pl.when(has_more)
            def _():
                rs_copy(t, q, twin, slot_in).wait_recv()
                part[t, :, cols] = (acc + rsin[slot_in, :, cols].astype(f32)).astype(bf16)

            @pl.when(jnp.logical_not(has_more))
            def _():
                part[t, :, cols] = acc.astype(bf16)
            rs_copy(t, q, mp, slot_in).start()

        left = 2 * (n - 1) - z - tau

        @pl.when((left >= 0) & (left < z))
        def _():
            pass_on(left, z < n - 1, left, m - 2)
        right = tau - z

        @pl.when((right > z) & (right < n))
        def _():
            pass_on(right, z > 0, n + right, m + 2)

    def unit(origins, tau, last):
        rows = pl.ds(0, 2 * bal * len(origins))

        def wait_rows(q):
            for o in origins:
                twin_copy(o, q).wait_recv()
        loop(CHUNKS, wait_rows)
        for i, o in enumerate(origins):
            top = 2 * bal * i
            for b in range(nblk):
                xs[b, top:top + bal, :] = mine[o, :, b * bd:(b + 1) * bd]
                xs[b, top + bal:top + 2 * bal, :] = sib[o, :, b * bd:(b + 1) * bd]

        steps = min(nj, CHUNKS)
        group, passes = nj // steps, CHUNKS // steps

        def columns(g):
            for i in range(group):
                j = g * group + i

                def picked(index):
                    return jnp.concatenate([xs[index[j, k], rows, :] for k in range(knz)], axis=1)
                gv = jnp.dot(picked(gi), gate[j], preferred_element_type=f32)
                uv = jnp.dot(picked(ui), up[j], preferred_element_type=f32)
                hid[j, rows, :] = (gv / (1.0 + jnp.exp(-gv)) * uv).astype(bf16)
            if last is not None:
                @pl.when(last)
                def _():
                    for i in range(passes):
                        take_all(tau + 1, g * passes + i, True)
        loop(steps, columns)

        def down_row(j):
            h = hid[j, rows, :]
            for i in range(0, knz, 4):
                w = jnp.concatenate([down[j * knz + i + e] for e in range(4)], axis=1)
                p = jnp.dot(h, w, preferred_element_type=f32)
                for e in range(4):
                    prod[j * knz + i + e, rows, :] = p[:, e * bd:(e + 1) * bd]
        loop(nj, down_row)

        def gather(q):
            def some(i):
                for e in range(2):
                    b = q * (nblk // CHUNKS) + 2 * i + e
                    acc = prod[inv[0, b], rows, :]
                    for j in range(1, nj):
                        acc += prod[inv[j, b], rows, :]
                    cols = pl.ds(pl.multiple_of(b * bd, bd), bd)
                    acc = acc.astype(bf16)
                    for r, o in enumerate(origins):
                        top = 2 * bal * r
                        part[o, :, cols] = acc[top:top + bal]
                        sibout[o, :, cols] = acc[top + bal:top + 2 * bal]
            loop(nblk // CHUNKS // 2, some)
            for o in origins:
                part_copy(o, q).start()
            if last is not None:
                @pl.when(last & (q > 0))
                def _():
                    hop(tau, q - 1)
        loop(CHUNKS, gather)
        if last is not None:
            @pl.when(last)
            def _():
                hop(tau, CHUNKS - 1)

    unit([z], 0, None)

    def phase(i):
        tau = i + 1

        @pl.when(tau > 1)
        def _():
            loop(CHUNKS, lambda q: take_all(tau, q, False))

        def side(i):
            o = z + (2 * i - 1) * tau

            @pl.when((o >= 0) & (o < n))
            def _():
                unit([o], tau, (i == 1) | (z + tau >= n))
        loop(2, side)

        @pl.when((z - tau < 0) & (z + tau >= n))
        def _():
            loop(CHUNKS, lambda q: hop(tau, q))
    loop(n - 1, phase)

    def finish(q):
        cols = cols_of(q)
        for s in range(1, ndp):
            exchange(sendp, recvp, x_s, x_r, s, q).wait_send()
        loop(n - 1, lambda i: hop(n + i, q))
        part_copy(z, q).wait_recv()
        total[...] = part[z, :, cols].astype(f32) + sibin[z, :, cols].astype(f32)

        @pl.when(z < n - 1)
        def _():
            rs_copy(z, q, twin, z).wait_recv()
            total[...] += rsin[z, :, cols].astype(f32)

        @pl.when(z > 0)
        def _():
            rs_copy(z, q, twin, n + z).wait_recv()
            total[...] += rsin[n + z, :, cols].astype(f32)
        sendp[:, cols] = jnp.dot(expand, total[...].astype(bf16), preferred_element_type=f32).astype(bf16)
        for s in range(1, ndp):
            exchange(sendp, back, bk_s, bk_r, s, q).start()
        back[slab(d), cols] = sendp[slab(d), cols]
    loop(CHUNKS, finish)

    def store(q):
        cols = cols_of(q)
        for s in range(1, ndp):
            arrived(sendp, back, bk_s, bk_r, s, q).wait_recv()
        out[:, cols] = jnp.dot(perm_t, back[:, cols], preferred_element_type=f32).astype(bf16)
    loop(CHUNKS, store)

    def drain(q):
        for s in range(1, ndp):
            exchange(sendp, back, bk_s, bk_r, s, q).wait_send()

        @pl.when(z > 0)
        def _():
            ag_copy(z, q, m - 2, n).wait_send()

        def each(o):
            twin_copy(o, q).wait_send()
            part_copy(o, q).wait_send()

            @pl.when(((o <= z) & (z < n - 1)) | ((o > z) & (z > 0)))
            def _():
                ag_copy(o, q, twin, o).wait_send()

            @pl.when(o != z)
            def _():
                rs_copy(o, q, twin, o).wait_send()
        loop(n, each)
    loop(CHUNKS, drain)


def body(tokens, row_counts, gate_blocks, gate_index, up_blocks, up_index, down_blocks, down_index):
    ndp, nmp = lax.axis_size("dp"), lax.axis_size("mp")
    n = nmp // 2
    rows_in, width = tokens.shape
    nj, knz, bd, bf = gate_blocks.shape
    nblk = width // bd
    bal = rows_in // 2
    sl = -(-(rows_in // ndp) // 16) * 16
    ids = jnp.arange(nj * knz, dtype=jnp.int32).reshape(nj, knz)
    hit = down_index[:, :, None] == jnp.arange(nblk, dtype=jnp.int32)
    inv = jnp.min(jnp.where(hit, ids[:, :, None], nj * knz), axis=1)
    bf16 = jnp.bfloat16
    vm, sm, hbm = (pl.BlockSpec(memory_space=s) for s in (pltpu.VMEM, pltpu.SMEM, pl.ANY))
    dma = pltpu.SemaphoreType.DMA
    rows = n * 2 * bal
    tall = 2 * bal
    return pl.pallas_call(
        functools.partial(kernel, ndp, n, sl),
        out_shape=jax.ShapeDtypeStruct(tokens.shape, bf16),
        in_specs=[vm, sm, hbm, sm, hbm, sm, hbm, sm],
        out_specs=vm,
        scratch_shapes=[
            pltpu.VMEM((nj, knz * bd, bf), bf16),
            pltpu.VMEM((nj, knz * bd, bf), bf16),
            pltpu.VMEM((nj * knz, bf, bd), bf16),
            pltpu.VMEM((ndp * sl, width), bf16),
            pltpu.VMEM((ndp * sl, width), bf16),
            pltpu.VMEM((n, bal, width), bf16),
            pltpu.VMEM((n, bal, width), bf16),
            pltpu.VMEM((nblk, tall, bd), bf16),
            pltpu.VMEM((nj, tall, bf), bf16),
            pltpu.VMEM((nj * knz + 1, tall, bd), jnp.float32),
            pltpu.VMEM((bal, width // CHUNKS), jnp.float32),
            pltpu.VMEM((n, bal, width), bf16),
            pltpu.VMEM((n, bal, width), bf16),
            pltpu.VMEM((n, bal, width), bf16),
            pltpu.VMEM((2 * n, bal, width), bf16),
            pltpu.VMEM((ndp * sl, width), bf16),
            dma((3,)),
            dma((ndp - 1, CHUNKS)), dma((ndp - 1, CHUNKS)),
            dma((n + 1, CHUNKS)), dma((n, CHUNKS)),
            dma((n, CHUNKS)), dma((n, CHUNKS)),
            dma((n, CHUNKS)), dma((n, CHUNKS)),
            dma((n, CHUNKS)), dma((2 * n, CHUNKS)),
            dma((ndp - 1, CHUNKS)), dma((ndp - 1, CHUNKS)),
        ],
        compiler_params=pltpu.CompilerParams(
            collective_id=0, has_side_effects=True, vmem_limit_bytes=60 * 1024 * 1024
        ),
        cost_estimate=pl.CostEstimate(
            flops=6 * rows * nj * knz * bd * bf, bytes_accessed=6 * nj * knz * bd * bf, transcendentals=rows * nj * bf
        ),
    )(
        tokens, row_counts, gate_blocks.reshape(nj, knz * bd, bf), gate_index,
        up_blocks.reshape(nj, knz * bd, bf), up_index, down_blocks.reshape(nj * knz, bf, bd), inv,
    )


def solution(mesh):
    in_specs = (
        P(("dp", "mp"), None),
        P(),
        P("mp", None, None, None),
        P("mp", None),
        P("mp", None, None, None),
        P("mp", None),
        P("mp", None, None, None),
        P("mp", None),
    )
    out_specs = P(("dp", "mp"), None)
    return jax.shard_map(body, mesh=mesh, in_specs=in_specs, out_specs=out_specs, check_vma=False)
```

```python
import functools

import jax
import jax.numpy as jnp
from jax import lax
from jax.experimental import pallas as pl
from jax.experimental.pallas import tpu as pltpu
from jax.sharding import PartitionSpec as P

MESH = pl.DeviceIdType.MESH
CHUNKS = 4


def kernel(
    ndp, n, sl,
    tok, cnt, gate_h, gi, up_h, ui, down_h, inv,
    out,
    gate, up, down, sendp, recvp, mine, sib, xs, hid, prod, total, part, sibout, sibin, rsin, back,
    w_sem, x_s, x_r, ag_s, ag_r, sb_s, sb_r, ps_s, ps_r, rs_s, rs_r, bk_s, bk_r,
):
    f32, bf16 = jnp.float32, jnp.bfloat16
    rows_in, width = tok.shape
    bal = mine.shape[1]
    nj, knz = gi.shape
    bf = gate.shape[2]
    bd = down.shape[2]
    nblk = inv.shape[1]
    ndown = down.shape[0]
    chunk = width // CHUNKS
    per_slab = rows_in // ndp
    d, m = lax.axis_index("dp"), lax.axis_index("mp")
    z, c = lax.div(m, 2), lax.rem(m, 2)
    twin = 2 * z + 1 - c

    def cols_of(q):
        return pl.ds(pl.multiple_of(q * chunk, chunk), chunk)

    def slab(s):
        return pl.ds(pl.multiple_of(s * sl, sl), sl)

    def loop(count, fn):
        def step(i, carry):
            fn(i)
            return carry
        lax.fori_loop(0, count, step, 0)

    def remote(src, dst, ssem, rsem, **where):
        return pltpu.make_async_remote_copy(
            src_ref=src, dst_ref=dst, send_sem=ssem, recv_sem=rsem, device_id=where, device_id_type=MESH
        )

    loads = [
        pltpu.make_async_copy(gate_h, gate, w_sem.at[0]),
        pltpu.make_async_copy(up_h, up, w_sem.at[1]),
        pltpu.make_async_copy(down_h, down, w_sem.at[2]),
    ]

    barrier = pltpu.get_barrier_semaphore()
    for s in range(1, ndp):
        pl.semaphore_signal(barrier, inc=1, device_id={"dp": lax.rem(d + s, ndp)}, device_id_type=MESH)
    pl.semaphore_signal(barrier, inc=1, device_id={"mp": twin}, device_id_type=MESH)

    @pl.when(z > 0)
    def _():
        pl.semaphore_signal(barrier, inc=1, device_id={"mp": m - 2}, device_id_type=MESH)

    @pl.when(z < n - 1)
    def _():
        pl.semaphore_signal(barrier, inc=1, device_id={"mp": m + 2}, device_id_type=MESH)

    place = lax.broadcasted_iota(jnp.int32, (ndp * sl, rows_in), 0)
    slot = lax.broadcasted_iota(jnp.int32, (ndp * sl, rows_in), 1)
    inner = lax.rem(place, sl)
    perm = ((slot == inner * ndp + lax.div(place, sl)) & (inner < per_slab)).astype(f32).astype(bf16)
    place_t = lax.broadcasted_iota(jnp.int32, (rows_in, ndp * sl), 1)
    slot_t = lax.broadcasted_iota(jnp.int32, (rows_in, ndp * sl), 0)
    inner_t = lax.rem(place_t, sl)
    perm_t = ((slot_t == inner_t * ndp + lax.div(place_t, sl)) & (inner_t < per_slab)).astype(f32).astype(bf16)

    row = lax.broadcasted_iota(jnp.int32, (bal, ndp * sl), 0)
    col = lax.broadcasted_iota(jnp.int32, (bal, ndp * sl), 1)
    row_t = lax.broadcasted_iota(jnp.int32, (ndp * sl, bal), 1)
    col_t = lax.broadcasted_iota(jnp.int32, (ndp * sl, bal), 0)
    compact = jnp.zeros((bal, ndp * sl), f32)
    expand = jnp.zeros((ndp * sl, bal), f32)
    first = jnp.int32(0)
    for s in range(ndp):
        valid = lax.div(cnt[s, m], ndp)
        low, high = s * sl, s * sl + valid
        compact += ((col >= low) & (col < high) & (row == col - low + first)).astype(f32)
        expand += ((col_t >= low) & (col_t < high) & (row_t == col_t - low + first)).astype(f32)
        first = first + valid
    compact, expand = compact.astype(bf16), expand.astype(bf16)

    def exchange(src, dst, ssem, rsem, s, q):
        peer = lax.rem(d + s, ndp)
        return remote(src.at[slab(peer), cols_of(q)], dst.at[slab(d), cols_of(q)],
                      ssem.at[s - 1, q], rsem.at[s - 1, q], dp=peer)

    def arrived(src, dst, ssem, rsem, s, q):
        peer = lax.rem(d + ndp - s, ndp)
        return remote(src.at[slab(peer), cols_of(q)], dst.at[slab(peer), cols_of(q)],
                      ssem.at[s - 1, q], rsem.at[s - 1, q], dp=peer)

    def ag_copy(o, q, mp, send_slot):
        ref = mine.at[o, :, cols_of(q)]
        return remote(ref, ref, ag_s.at[send_slot, q], ag_r.at[o, q], mp=mp)

    def twin_copy(o, q):
        return remote(mine.at[o, :, cols_of(q)], sib.at[o, :, cols_of(q)], sb_s.at[o, q], sb_r.at[o, q], mp=twin)

    def part_copy(o, q):
        return remote(sibout.at[o, :, cols_of(q)], sibin.at[o, :, cols_of(q)], ps_s.at[o, q], ps_r.at[o, q], mp=twin)

    def rs_copy(t, q, mp, dst_slot):
        return remote(part.at[t, :, cols_of(q)], rsin.at[dst_slot, :, cols_of(q)],
                      rs_s.at[t, q], rs_r.at[dst_slot, q], mp=mp)

    at_end = (z == 0) | (z == n - 1)

    @pl.when(at_end)
    def _():
        pl.semaphore_wait(barrier, ndp + min(n - 1, 1))

    @pl.when(jnp.logical_not(at_end))
    def _():
        pl.semaphore_wait(barrier, ndp + 2)

    def send_tokens(q):
        cols = cols_of(q)
        sendp[:, cols] = jnp.dot(perm, tok[:, cols], preferred_element_type=f32).astype(bf16)
        for s in range(1, ndp):
            exchange(sendp, recvp, x_s, x_r, s, q).start()
        recvp[slab(d), cols] = sendp[slab(d), cols]
    loop(CHUNKS, send_tokens)
    for load in loads:
        load.start()
    prod[ndown] = jnp.zeros(prod.shape[1:], f32)

    def take(o, q, sign):
        ag_copy(o, q, twin, o).wait_recv()
        beyond = z - sign

        @pl.when((beyond >= 0) & (beyond < n))
        def _():
            ag_copy(o, q, m - 2 * sign, o).start()
        twin_copy(o, q).start()

    def take_all(tau, q, passing):
        for sign in (-1, 1):
            o, beyond = z + sign * tau, z - sign
            inside = (beyond >= 0) & (beyond < n)
            wanted = inside if passing else jnp.logical_not(inside)

            @pl.when((o >= 0) & (o < n) & wanted)
            def _():
                take(o, q, sign)

    def spread(q):
        cols = cols_of(q)
        for s in range(1, ndp):
            arrived(sendp, recvp, x_s, x_r, s, q).wait_recv()
        mine[z, :, cols] = jnp.dot(compact, recvp[:, cols], preferred_element_type=f32).astype(bf16)

        @pl.when(z < n - 1)
        def _():
            ag_copy(z, q, m + 2, z).start()

        @pl.when(z > 0)
        def _():
            ag_copy(z, q, m - 2, n).start()
        twin_copy(z, q).start()
    loop(CHUNKS, spread)
    for load in loads:
        load.wait()

    def hop(tau, q):
        cols = cols_of(q)

        def pass_on(t, has_more, slot_in, mp):
            part_copy(t, q).wait_recv()
            acc = part[t, :, cols].astype(f32) + sibin[t, :, cols].astype(f32)

            @pl.when(has_more)
            def _():
                rs_copy(t, q, twin, slot_in).wait_recv()
                part[t, :, cols] = (acc + rsin[slot_in, :, cols].astype(f32)).astype(bf16)

            @pl.when(jnp.logical_not(has_more))
            def _():
                part[t, :, cols] = acc.astype(bf16)
            rs_copy(t, q, mp, slot_in).start()

        left = 2 * (n - 1) - z - tau

        @pl.when((left >= 0) & (left < z))
        def _():
            pass_on(left, z < n - 1, left, m - 2)
        right = tau - z

        @pl.when((right > z) & (right < n))
        def _():
            pass_on(right, z > 0, n + right, m + 2)

    def unit(origins, tau, last):
        rows = pl.ds(0, 2 * bal * len(origins))

        def wait_rows(q):
            for o in origins:
                twin_copy(o, q).wait_recv()
        loop(CHUNKS, wait_rows)
        for i, o in enumerate(origins):
            top = 2 * bal * i
            for b in range(nblk):
                xs[b, top:top + bal, :] = mine[o, :, b * bd:(b + 1) * bd]
                xs[b, top + bal:top + 2 * bal, :] = sib[o, :, b * bd:(b + 1) * bd]

        steps = min(nj, CHUNKS)
        group, passes = nj // steps, CHUNKS // steps

        def columns(g):
            for i in range(group):
                j = g * group + i

                def picked(index):
                    return jnp.concatenate([xs[index[j, k], rows, :] for k in range(knz)], axis=1)
                gv = jnp.dot(picked(gi), gate[j], preferred_element_type=f32)
                uv = jnp.dot(picked(ui), up[j], preferred_element_type=f32)
                hid[j, rows, :] = (gv / (1.0 + jnp.exp(-gv)) * uv).astype(bf16)

            @pl.when(last)
            def _():
                for i in range(passes):
                    take_all(tau + 1, g * passes + i, True)
        loop(steps, columns)

        def down_row(j):
            h = hid[j, rows, :]
            for i in range(0, knz, 2):
                w = jnp.concatenate([down[j * knz + i + e] for e in range(2)], axis=1)
                p = jnp.dot(h, w, preferred_element_type=f32)
                for e in range(2):
                    prod[j * knz + i + e, rows, :] = p[:, e * bd:(e + 1) * bd]
        loop(nj, down_row)

        def gather(q):
            def some(i):
                for e in range(2):
                    b = q * (nblk // CHUNKS) + 2 * i + e
                    acc = prod[inv[0, b], rows, :]
                    for j in range(1, nj):
                        acc += prod[inv[j, b], rows, :]
                    cols = pl.ds(pl.multiple_of(b * bd, bd), bd)
                    acc = acc.astype(bf16)
                    for r, o in enumerate(origins):
                        top = 2 * bal * r
                        part[o, :, cols] = acc[top:top + bal]
                        sibout[o, :, cols] = acc[top + bal:top + 2 * bal]
            loop(nblk // CHUNKS // 2, some)
            for o in origins:
                part_copy(o, q).start()
        loop(CHUNKS, gather)

    unit([z], 0, z >= 0)

    def phase(i):
        tau = i + 1
        loop(CHUNKS, lambda q: take_all(tau, q, False))

        def side(i):
            o = z + (2 * i - 1) * tau

            @pl.when((o >= 0) & (o < n))
            def _():
                unit([o], tau, (i == 1) | (z + tau >= n))
        loop(2, side)
        loop(CHUNKS, lambda q: hop(tau, q))
    loop(n - 1, phase)

    def finish(q):
        cols = cols_of(q)
        for s in range(1, ndp):
            exchange(sendp, recvp, x_s, x_r, s, q).wait_send()
        part_copy(z, q).wait_recv()
        total[...] = part[z, :, cols].astype(f32) + sibin[z, :, cols].astype(f32)

        @pl.when(z < n - 1)
        def _():
            rs_copy(z, q, twin, z).wait_recv()
            total[...] += rsin[z, :, cols].astype(f32)

        @pl.when(z > 0)
        def _():
            rs_copy(z, q, twin, n + z).wait_recv()
            total[...] += rsin[n + z, :, cols].astype(f32)
        sendp[:, cols] = jnp.dot(expand, total[...].astype(bf16), preferred_element_type=f32).astype(bf16)
        for s in range(1, ndp):
            exchange(sendp, back, bk_s, bk_r, s, q).start()
        back[slab(d), cols] = sendp[slab(d), cols]

    def tail(turn):
        for i in range(n - 1):
            q = turn - i

            @pl.when((q >= 0) & (q < CHUNKS))
            def _():
                hop(n + i, q)
        q = turn - (n - 1)

        @pl.when(q >= 0)
        def _():
            finish(q)
    loop(CHUNKS + n - 1, tail)

    def store(q):
        cols = cols_of(q)
        for s in range(1, ndp):
            arrived(sendp, back, bk_s, bk_r, s, q).wait_recv()
        out[:, cols] = jnp.dot(perm_t, back[:, cols], preferred_element_type=f32).astype(bf16)
    loop(CHUNKS, store)

    def drain(q):
        for s in range(1, ndp):
            exchange(sendp, back, bk_s, bk_r, s, q).wait_send()

        @pl.when(z > 0)
        def _():
            ag_copy(z, q, m - 2, n).wait_send()

        def each(o):
            twin_copy(o, q).wait_send()
            part_copy(o, q).wait_send()

            @pl.when(((o <= z) & (z < n - 1)) | ((o > z) & (z > 0)))
            def _():
                ag_copy(o, q, twin, o).wait_send()

            @pl.when(o != z)
            def _():
                rs_copy(o, q, twin, o).wait_send()
        loop(n, each)
    loop(CHUNKS, drain)


def body(tokens, row_counts, gate_blocks, gate_index, up_blocks, up_index, down_blocks, down_index):
    ndp, nmp = lax.axis_size("dp"), lax.axis_size("mp")
    n = nmp // 2
    rows_in, width = tokens.shape
    nj, knz, bd, bf = gate_blocks.shape
    nblk = width // bd
    bal = rows_in // 2
    sl = -(-(rows_in // ndp) // 16) * 16
    ids = jnp.arange(nj * knz, dtype=jnp.int32).reshape(nj, knz)
    hit = down_index[:, :, None] == jnp.arange(nblk, dtype=jnp.int32)
    inv = jnp.min(jnp.where(hit, ids[:, :, None], nj * knz), axis=1)
    bf16 = jnp.bfloat16
    vm, sm, hbm = (pl.BlockSpec(memory_space=s) for s in (pltpu.VMEM, pltpu.SMEM, pl.ANY))
    dma = pltpu.SemaphoreType.DMA
    rows = n * 2 * bal
    tall = 2 * bal
    return pl.pallas_call(
        functools.partial(kernel, ndp, n, sl),
        out_shape=jax.ShapeDtypeStruct(tokens.shape, bf16),
        in_specs=[vm, sm, hbm, sm, hbm, sm, hbm, sm],
        out_specs=vm,
        scratch_shapes=[
            pltpu.VMEM((nj, knz * bd, bf), bf16),
            pltpu.VMEM((nj, knz * bd, bf), bf16),
            pltpu.VMEM((nj * knz, bf, bd), bf16),
            pltpu.VMEM((ndp * sl, width), bf16),
            pltpu.VMEM((ndp * sl, width), bf16),
            pltpu.VMEM((n, bal, width), bf16),
            pltpu.VMEM((n, bal, width), bf16),
            pltpu.VMEM((nblk, tall, bd), bf16),
            pltpu.VMEM((nj, tall, bf), bf16),
            pltpu.VMEM((nj * knz + 1, tall, bd), jnp.float32),
            pltpu.VMEM((bal, width // CHUNKS), jnp.float32),
            pltpu.VMEM((n, bal, width), bf16),
            pltpu.VMEM((n, bal, width), bf16),
            pltpu.VMEM((n, bal, width), bf16),
            pltpu.VMEM((2 * n, bal, width), bf16),
            pltpu.VMEM((ndp * sl, width), bf16),
            dma((3,)),
            dma((ndp - 1, CHUNKS)), dma((ndp - 1, CHUNKS)),
            dma((n + 1, CHUNKS)), dma((n, CHUNKS)),
            dma((n, CHUNKS)), dma((n, CHUNKS)),
            dma((n, CHUNKS)), dma((n, CHUNKS)),
            dma((n, CHUNKS)), dma((2 * n, CHUNKS)),
            dma((ndp - 1, CHUNKS)), dma((ndp - 1, CHUNKS)),
        ],
        compiler_params=pltpu.CompilerParams(
            collective_id=0, has_side_effects=True, vmem_limit_bytes=60 * 1024 * 1024
        ),
        cost_estimate=pl.CostEstimate(
            flops=6 * rows * nj * knz * bd * bf, bytes_accessed=6 * nj * knz * bd * bf, transcendentals=rows * nj * bf
        ),
    )(
        tokens, row_counts, gate_blocks.reshape(nj, knz * bd, bf), gate_index,
        up_blocks.reshape(nj, knz * bd, bf), up_index, down_blocks.reshape(nj * knz, bf, bd), inv,
    )


def solution(mesh):
    in_specs = (
        P(("dp", "mp"), None),
        P(),
        P("mp", None, None, None),
        P("mp", None),
        P("mp", None, None, None),
        P("mp", None),
        P("mp", None, None, None),
        P("mp", None),
    )
    out_specs = P(("dp", "mp"), None)
    return jax.shard_map(body, mesh=mesh, in_specs=in_specs, out_specs=out_specs, check_vma=False)
```

```python
import functools

import jax
import jax.numpy as jnp
from jax import lax
from jax.experimental import pallas as pl
from jax.experimental.pallas import tpu as pltpu
from jax.sharding import PartitionSpec as P

MESH = pl.DeviceIdType.MESH
CHUNKS = 8
SKEW = 2


def kernel(
    ndp, n, sl,
    tok, cnt, gate_h, gi, up_h, ui, down_h, inv,
    out,
    gate, up, down, sendp, recvp, mine, sib, xs, hid, prod, total, part, sibout, sibin, rsin, back,
    w_sem, x_s, x_r, ag_s, ag_r, sb_s, sb_r, ps_s, ps_r, rs_s, rs_r, bk_s, bk_r,
):
    f32, bf16 = jnp.float32, jnp.bfloat16
    rows_in, width = tok.shape
    bal = mine.shape[1]
    nj, knz = gi.shape
    bf = gate.shape[2]
    bd = down.shape[2]
    nblk = inv.shape[1]
    ndown = down.shape[0]
    chunk = width // CHUNKS
    per_slab = rows_in // ndp
    d, m = lax.axis_index("dp"), lax.axis_index("mp")
    z, c = lax.div(m, 2), lax.rem(m, 2)
    twin = 2 * z + 1 - c

    def cols_of(q):
        return pl.ds(pl.multiple_of(q * chunk, chunk), chunk)

    def slab(s):
        return pl.ds(pl.multiple_of(s * sl, sl), sl)

    def loop(count, fn):
        def step(i, carry):
            fn(i)
            return carry
        lax.fori_loop(0, count, step, 0)

    def remote(src, dst, ssem, rsem, **where):
        return pltpu.make_async_remote_copy(
            src_ref=src, dst_ref=dst, send_sem=ssem, recv_sem=rsem, device_id=where, device_id_type=MESH
        )

    loads = [
        pltpu.make_async_copy(gate_h, gate, w_sem.at[0]),
        pltpu.make_async_copy(up_h, up, w_sem.at[1]),
        pltpu.make_async_copy(down_h, down, w_sem.at[2]),
    ]

    barrier = pltpu.get_barrier_semaphore()
    for s in range(1, ndp):
        pl.semaphore_signal(barrier, inc=1, device_id={"dp": lax.rem(d + s, ndp)}, device_id_type=MESH)
    pl.semaphore_signal(barrier, inc=1, device_id={"mp": twin}, device_id_type=MESH)

    @pl.when(z > 0)
    def _():
        pl.semaphore_signal(barrier, inc=1, device_id={"mp": m - 2}, device_id_type=MESH)

    @pl.when(z < n - 1)
    def _():
        pl.semaphore_signal(barrier, inc=1, device_id={"mp": m + 2}, device_id_type=MESH)

    place = lax.broadcasted_iota(jnp.int32, (ndp * sl, rows_in), 0)
    slot = lax.broadcasted_iota(jnp.int32, (ndp * sl, rows_in), 1)
    inner = lax.rem(place, sl)
    perm = ((slot == inner * ndp + lax.div(place, sl)) & (inner < per_slab)).astype(f32).astype(bf16)
    place_t = lax.broadcasted_iota(jnp.int32, (rows_in, ndp * sl), 1)
    slot_t = lax.broadcasted_iota(jnp.int32, (rows_in, ndp * sl), 0)
    inner_t = lax.rem(place_t, sl)
    perm_t = ((slot_t == inner_t * ndp + lax.div(place_t, sl)) & (inner_t < per_slab)).astype(f32).astype(bf16)

    row = lax.broadcasted_iota(jnp.int32, (bal, ndp * sl), 0)
    col = lax.broadcasted_iota(jnp.int32, (bal, ndp * sl), 1)
    row_t = lax.broadcasted_iota(jnp.int32, (ndp * sl, bal), 1)
    col_t = lax.broadcasted_iota(jnp.int32, (ndp * sl, bal), 0)
    compact = jnp.zeros((bal, ndp * sl), f32)
    expand = jnp.zeros((ndp * sl, bal), f32)
    first = jnp.int32(0)
    for s in range(ndp):
        valid = lax.div(cnt[s, m], ndp)
        low, high = s * sl, s * sl + valid
        compact += ((col >= low) & (col < high) & (row == col - low + first)).astype(f32)
        expand += ((col_t >= low) & (col_t < high) & (row_t == col_t - low + first)).astype(f32)
        first = first + valid
    compact, expand = compact.astype(bf16), expand.astype(bf16)

    def exchange(src, dst, ssem, rsem, s, q):
        peer = lax.rem(d + s, ndp)
        return remote(src.at[slab(peer), cols_of(q)], dst.at[slab(d), cols_of(q)],
                      ssem.at[s - 1, q], rsem.at[s - 1, q], dp=peer)

    def arrived(src, dst, ssem, rsem, s, q):
        peer = lax.rem(d + ndp - s, ndp)
        return remote(src.at[slab(peer), cols_of(q)], dst.at[slab(peer), cols_of(q)],
                      ssem.at[s - 1, q], rsem.at[s - 1, q], dp=peer)

    def ag_copy(o, q, mp, send_slot):
        ref = mine.at[o, :, cols_of(q)]
        return remote(ref, ref, ag_s.at[send_slot, q], ag_r.at[o, q], mp=mp)

    def twin_copy(o, q):
        return remote(mine.at[o, :, cols_of(q)], sib.at[o, :, cols_of(q)], sb_s.at[o, q], sb_r.at[o, q], mp=twin)

    def part_copy(o, q):
        return remote(sibout.at[o, :, cols_of(q)], sibin.at[o, :, cols_of(q)], ps_s.at[o, q], ps_r.at[o, q], mp=twin)

    def rs_copy(t, q, mp, dst_slot):
        return remote(part.at[t, :, cols_of(q)], rsin.at[dst_slot, :, cols_of(q)],
                      rs_s.at[t, q], rs_r.at[dst_slot, q], mp=mp)

    at_end = (z == 0) | (z == n - 1)

    @pl.when(at_end)
    def _():
        pl.semaphore_wait(barrier, ndp + min(n - 1, 1))

    @pl.when(jnp.logical_not(at_end))
    def _():
        pl.semaphore_wait(barrier, ndp + 2)

    def send_tokens(q):
        cols = cols_of(q)
        sendp[:, cols] = jnp.dot(perm, tok[:, cols], preferred_element_type=f32).astype(bf16)
        for s in range(1, ndp):
            exchange(sendp, recvp, x_s, x_r, s, q).start()
        recvp[slab(d), cols] = sendp[slab(d), cols]
    loop(CHUNKS, send_tokens)
    for load in loads:
        load.start()
    prod[ndown] = jnp.zeros(prod.shape[1:], f32)

    def take(o, q, sign):
        ag_copy(o, q, twin, o).wait_recv()
        beyond = z - sign

        @pl.when((beyond >= 0) & (beyond < n))
        def _():
            ag_copy(o, q, m - 2 * sign, o).start()
        twin_copy(o, q).start()

    def take_all(tau, q, passing):
        for sign in (-1, 1):
            o, beyond = z + sign * tau, z - sign
            inside = (beyond >= 0) & (beyond < n)
            wanted = inside if passing else jnp.logical_not(inside)

            @pl.when((o >= 0) & (o < n) & wanted)
            def _():
                take(o, q, sign)

    def spread(q):
        cols = cols_of(q)
        for s in range(1, ndp):
            arrived(sendp, recvp, x_s, x_r, s, q).wait_recv()
        mine[z, :, cols] = jnp.dot(compact, recvp[:, cols], preferred_element_type=f32).astype(bf16)

        @pl.when(z < n - 1)
        def _():
            ag_copy(z, q, m + 2, z).start()

        @pl.when(z > 0)
        def _():
            ag_copy(z, q, m - 2, n).start()
        twin_copy(z, q).start()
    loop(CHUNKS, spread)
    for load in loads:
        load.wait()

    def hop(tau, q):
        cols = cols_of(q)

        def pass_on(t, has_more, slot_in, mp):
            part_copy(t, q).wait_recv()
            acc = part[t, :, cols].astype(f32) + sibin[t, :, cols].astype(f32)

            @pl.when(has_more)
            def _():
                rs_copy(t, q, twin, slot_in).wait_recv()
                part[t, :, cols] = (acc + rsin[slot_in, :, cols].astype(f32)).astype(bf16)

            @pl.when(jnp.logical_not(has_more))
            def _():
                part[t, :, cols] = acc.astype(bf16)
            rs_copy(t, q, mp, slot_in).start()

        left = 2 * (n - 1) - z - tau

        @pl.when((left >= 0) & (left < z))
        def _():
            pass_on(left, z < n - 1, left, m - 2)
        right = tau - z

        @pl.when((right > z) & (right < n))
        def _():
            pass_on(right, z > 0, n + right, m + 2)

    def unit(origins, tau, passing):
        rows = pl.ds(0, 2 * bal * len(origins))

        def wait_rows(q):
            for o in origins:
                twin_copy(o, q).wait_recv()
        loop(CHUNKS, wait_rows)
        for i, o in enumerate(origins):
            top = 2 * bal * i
            for b in range(nblk):
                xs[b, top:top + bal, :] = mine[o, :, b * bd:(b + 1) * bd]
                xs[b, top + bal:top + 2 * bal, :] = sib[o, :, b * bd:(b + 1) * bd]

        steps = min(nj, CHUNKS)
        group, passes = nj // steps, CHUNKS // steps

        def columns(g):
            for i in range(group):
                j = g * group + i

                def picked(index):
                    return jnp.concatenate([xs[index[j, k], rows, :] for k in range(knz)], axis=1)
                gv = jnp.dot(picked(gi), gate[j], preferred_element_type=f32)
                uv = jnp.dot(picked(ui), up[j], preferred_element_type=f32)
                hid[j, rows, :] = (gv / (1.0 + jnp.exp(-gv)) * uv).astype(bf16)

            @pl.when(passing)
            def _():
                for i in range(passes):
                    take_all(tau + 1, g * passes + i, True)
        loop(steps, columns)

        def down_row(j):
            h = hid[j, rows, :]
            for i in range(0, knz, 2):
                w = jnp.concatenate([down[j * knz + i + e] for e in range(2)], axis=1)
                p = jnp.dot(h, w, preferred_element_type=f32)
                for e in range(2):
                    prod[j * knz + i + e, rows, :] = p[:, e * bd:(e + 1) * bd]
        loop(nj, down_row)

        def gather(q):
            def some(i):
                for e in range(2):
                    b = q * (nblk // CHUNKS) + 2 * i + e
                    acc = prod[inv[0, b], rows, :]
                    for j in range(1, nj):
                        acc += prod[inv[j, b], rows, :]
                    cols = pl.ds(pl.multiple_of(b * bd, bd), bd)
                    acc = acc.astype(bf16)
                    for r, o in enumerate(origins):
                        top = 2 * bal * r
                        part[o, :, cols] = acc[top:top + bal]
                        sibout[o, :, cols] = acc[top + bal:top + 2 * bal]
            loop(nblk // CHUNKS // 2, some)
            for o in origins:
                part_copy(o, q).start()
        loop(CHUNKS, gather)

    unit([z], 0, z >= 0)

    def phase(i):
        tau = i + 1
        loop(CHUNKS, lambda q: take_all(tau, q, False))

        def side(i):
            o = z + (2 * i - 1) * tau

            @pl.when((o >= 0) & (o < n))
            def _():
                unit([o], tau, (i == 0) | (z - tau < 0))
        loop(2, side)
        loop(CHUNKS, lambda q: hop(tau, q))
    loop(n - 1, phase)

    def finish(q):
        cols = cols_of(q)
        for s in range(1, ndp):
            exchange(sendp, recvp, x_s, x_r, s, q).wait_send()
        part_copy(z, q).wait_recv()
        total[...] = part[z, :, cols].astype(f32) + sibin[z, :, cols].astype(f32)

        @pl.when(z < n - 1)
        def _():
            rs_copy(z, q, twin, z).wait_recv()
            total[...] += rsin[z, :, cols].astype(f32)

        @pl.when(z > 0)
        def _():
            rs_copy(z, q, twin, n + z).wait_recv()
            total[...] += rsin[n + z, :, cols].astype(f32)
        sendp[:, cols] = jnp.dot(expand, total[...].astype(bf16), preferred_element_type=f32).astype(bf16)
        for s in range(1, ndp):
            exchange(sendp, back, bk_s, bk_r, s, q).start()
        back[slab(d), cols] = sendp[slab(d), cols]

    def tail(turn):
        for i in range(n - 2):
            q = turn - i * SKEW

            @pl.when((q >= 0) & (q < CHUNKS))
            def _():
                hop(n + i, q)
        q = turn - (n - 2) * SKEW

        @pl.when(q >= 0)
        def _():
            finish(q)
    loop(CHUNKS + (n - 2) * SKEW, tail)

    def store(q):
        cols = cols_of(q)
        for s in range(1, ndp):
            arrived(sendp, back, bk_s, bk_r, s, q).wait_recv()
        out[:, cols] = jnp.dot(perm_t, back[:, cols], preferred_element_type=f32).astype(bf16)
    loop(CHUNKS, store)

    def drain(q):
        for s in range(1, ndp):
            exchange(sendp, back, bk_s, bk_r, s, q).wait_send()

        @pl.when(z > 0)
        def _():
            ag_copy(z, q, m - 2, n).wait_send()

        def each(o):
            twin_copy(o, q).wait_send()
            part_copy(o, q).wait_send()

            @pl.when(((o <= z) & (z < n - 1)) | ((o > z) & (z > 0)))
            def _():
                ag_copy(o, q, twin, o).wait_send()

            @pl.when(o != z)
            def _():
                rs_copy(o, q, twin, o).wait_send()
        loop(n, each)
    loop(CHUNKS, drain)


def body(tokens, row_counts, gate_blocks, gate_index, up_blocks, up_index, down_blocks, down_index):
    ndp, nmp = lax.axis_size("dp"), lax.axis_size("mp")
    n = nmp // 2
    rows_in, width = tokens.shape
    nj, knz, bd, bf = gate_blocks.shape
    nblk = width // bd
    bal = rows_in // 2
    sl = -(-(rows_in // ndp) // 16) * 16
    ids = jnp.arange(nj * knz, dtype=jnp.int32).reshape(nj, knz)
    hit = down_index[:, :, None] == jnp.arange(nblk, dtype=jnp.int32)
    inv = jnp.min(jnp.where(hit, ids[:, :, None], nj * knz), axis=1)
    bf16 = jnp.bfloat16
    vm, sm, hbm = (pl.BlockSpec(memory_space=s) for s in (pltpu.VMEM, pltpu.SMEM, pl.ANY))
    dma = pltpu.SemaphoreType.DMA
    rows = n * 2 * bal
    tall = 2 * bal
    return pl.pallas_call(
        functools.partial(kernel, ndp, n, sl),
        out_shape=jax.ShapeDtypeStruct(tokens.shape, bf16),
        in_specs=[vm, sm, hbm, sm, hbm, sm, hbm, sm],
        out_specs=vm,
        scratch_shapes=[
            pltpu.VMEM((nj, knz * bd, bf), bf16),
            pltpu.VMEM((nj, knz * bd, bf), bf16),
            pltpu.VMEM((nj * knz, bf, bd), bf16),
            pltpu.VMEM((ndp * sl, width), bf16),
            pltpu.VMEM((ndp * sl, width), bf16),
            pltpu.VMEM((n, bal, width), bf16),
            pltpu.VMEM((n, bal, width), bf16),
            pltpu.VMEM((nblk, tall, bd), bf16),
            pltpu.VMEM((nj, tall, bf), bf16),
            pltpu.VMEM((nj * knz + 1, tall, bd), jnp.float32),
            pltpu.VMEM((bal, width // CHUNKS), jnp.float32),
            pltpu.VMEM((n, bal, width), bf16),
            pltpu.VMEM((n, bal, width), bf16),
            pltpu.VMEM((n, bal, width), bf16),
            pltpu.VMEM((2 * n, bal, width), bf16),
            pltpu.VMEM((ndp * sl, width), bf16),
            dma((3,)),
            dma((ndp - 1, CHUNKS)), dma((ndp - 1, CHUNKS)),
            dma((n + 1, CHUNKS)), dma((n, CHUNKS)),
            dma((n, CHUNKS)), dma((n, CHUNKS)),
            dma((n, CHUNKS)), dma((n, CHUNKS)),
            dma((n, CHUNKS)), dma((2 * n, CHUNKS)),
            dma((ndp - 1, CHUNKS)), dma((ndp - 1, CHUNKS)),
        ],
        compiler_params=pltpu.CompilerParams(
            collective_id=0, has_side_effects=True, vmem_limit_bytes=60 * 1024 * 1024
        ),
        cost_estimate=pl.CostEstimate(
            flops=6 * rows * nj * knz * bd * bf, bytes_accessed=6 * nj * knz * bd * bf, transcendentals=rows * nj * bf
        ),
    )(
        tokens, row_counts, gate_blocks.reshape(nj, knz * bd, bf), gate_index,
        up_blocks.reshape(nj, knz * bd, bf), up_index, down_blocks.reshape(nj * knz, bf, bd), inv,
    )


def solution(mesh):
    in_specs = (
        P(("dp", "mp"), None),
        P(),
        P("mp", None, None, None),
        P("mp", None),
        P("mp", None, None, None),
        P("mp", None),
        P("mp", None, None, None),
        P("mp", None),
    )
    out_specs = P(("dp", "mp"), None)
    return jax.shard_map(body, mesh=mesh, in_specs=in_specs, out_specs=out_specs, check_vma=False)
```

```python
import functools

import jax
import jax.numpy as jnp
from jax import lax
from jax.experimental import pallas as pl
from jax.experimental.pallas import tpu as pltpu
from jax.sharding import PartitionSpec as P

MESH = pl.DeviceIdType.MESH
CHUNKS = 4
SKEW = 1


def kernel(
    ndp, n, sl,
    tok, cnt, gate_h, gi, up_h, ui, down_h, inv,
    out,
    gate, up, down, sendp, recvp, mine, sib, xs, hid, prod, total, part, sibout, sibin, rsin, back,
    w_sem, x_s, x_r, ag_s, ag_r, sb_s, sb_r, ps_s, ps_r, rs_s, rs_r, bk_s, bk_r,
):
    f32, bf16 = jnp.float32, jnp.bfloat16
    rows_in, width = tok.shape
    bal = mine.shape[1]
    nj, knz = gi.shape
    bf = gate.shape[2]
    bd = down.shape[2]
    nblk = inv.shape[1]
    ndown = down.shape[0]
    chunk = width // CHUNKS
    per_slab = rows_in // ndp
    d, m = lax.axis_index("dp"), lax.axis_index("mp")
    z, c = lax.div(m, 2), lax.rem(m, 2)
    twin = 2 * z + 1 - c

    def cols_of(q):
        return pl.ds(pl.multiple_of(q * chunk, chunk), chunk)

    def slab(s):
        return pl.ds(pl.multiple_of(s * sl, sl), sl)

    def loop(count, fn):
        def step(i, carry):
            fn(i)
            return carry
        lax.fori_loop(0, count, step, 0)

    def remote(src, dst, ssem, rsem, **where):
        return pltpu.make_async_remote_copy(
            src_ref=src, dst_ref=dst, send_sem=ssem, recv_sem=rsem, device_id=where, device_id_type=MESH
        )

    loads = [
        pltpu.make_async_copy(gate_h, gate, w_sem.at[0]),
        pltpu.make_async_copy(up_h, up, w_sem.at[1]),
        pltpu.make_async_copy(down_h, down, w_sem.at[2]),
    ]

    barrier = pltpu.get_barrier_semaphore()
    for s in range(1, ndp):
        pl.semaphore_signal(barrier, inc=1, device_id={"dp": lax.rem(d + s, ndp)}, device_id_type=MESH)
    pl.semaphore_signal(barrier, inc=1, device_id={"mp": twin}, device_id_type=MESH)

    @pl.when(z > 0)
    def _():
        pl.semaphore_signal(barrier, inc=1, device_id={"mp": m - 2}, device_id_type=MESH)

    @pl.when(z < n - 1)
    def _():
        pl.semaphore_signal(barrier, inc=1, device_id={"mp": m + 2}, device_id_type=MESH)

    place = lax.broadcasted_iota(jnp.int32, (ndp * sl, rows_in), 0)
    slot = lax.broadcasted_iota(jnp.int32, (ndp * sl, rows_in), 1)
    inner = lax.rem(place, sl)
    perm = ((slot == inner * ndp + lax.div(place, sl)) & (inner < per_slab)).astype(f32).astype(bf16)
    place_t = lax.broadcasted_iota(jnp.int32, (rows_in, ndp * sl), 1)
    slot_t = lax.broadcasted_iota(jnp.int32, (rows_in, ndp * sl), 0)
    inner_t = lax.rem(place_t, sl)
    perm_t = ((slot_t == inner_t * ndp + lax.div(place_t, sl)) & (inner_t < per_slab)).astype(f32).astype(bf16)

    row = lax.broadcasted_iota(jnp.int32, (bal, ndp * sl), 0)
    col = lax.broadcasted_iota(jnp.int32, (bal, ndp * sl), 1)
    row_t = lax.broadcasted_iota(jnp.int32, (ndp * sl, bal), 1)
    col_t = lax.broadcasted_iota(jnp.int32, (ndp * sl, bal), 0)
    compact = jnp.zeros((bal, ndp * sl), f32)
    expand = jnp.zeros((ndp * sl, bal), f32)
    first = jnp.int32(0)
    for s in range(ndp):
        valid = lax.div(cnt[s, m], ndp)
        low, high = s * sl, s * sl + valid
        compact += ((col >= low) & (col < high) & (row == col - low + first)).astype(f32)
        expand += ((col_t >= low) & (col_t < high) & (row_t == col_t - low + first)).astype(f32)
        first = first + valid
    compact, expand = compact.astype(bf16), expand.astype(bf16)

    def exchange(src, dst, ssem, rsem, s, q):
        peer = lax.rem(d + s, ndp)
        return remote(src.at[slab(peer), cols_of(q)], dst.at[slab(d), cols_of(q)],
                      ssem.at[s - 1, q], rsem.at[s - 1, q], dp=peer)

    def arrived(src, dst, ssem, rsem, s, q):
        peer = lax.rem(d + ndp - s, ndp)
        return remote(src.at[slab(peer), cols_of(q)], dst.at[slab(peer), cols_of(q)],
                      ssem.at[s - 1, q], rsem.at[s - 1, q], dp=peer)

    def ag_copy(o, q, mp, send_slot):
        ref = mine.at[o, :, cols_of(q)]
        return remote(ref, ref, ag_s.at[send_slot, q], ag_r.at[o, q], mp=mp)

    def twin_copy(o, q):
        return remote(mine.at[o, :, cols_of(q)], sib.at[o, :, cols_of(q)], sb_s.at[o, q], sb_r.at[o, q], mp=twin)

    def part_copy(o, q):
        return remote(sibout.at[o, :, cols_of(q)], sibin.at[o, :, cols_of(q)], ps_s.at[o, q], ps_r.at[o, q], mp=twin)

    def rs_copy(t, q, mp, dst_slot):
        return remote(part.at[t, :, cols_of(q)], rsin.at[dst_slot, :, cols_of(q)],
                      rs_s.at[t, q], rs_r.at[dst_slot, q], mp=mp)

    at_end = (z == 0) | (z == n - 1)

    @pl.when(at_end)
    def _():
        pl.semaphore_wait(barrier, ndp + min(n - 1, 1))

    @pl.when(jnp.logical_not(at_end))
    def _():
        pl.semaphore_wait(barrier, ndp + 2)

    def send_tokens(q):
        cols = cols_of(q)
        sendp[:, cols] = jnp.dot(perm, tok[:, cols], preferred_element_type=f32).astype(bf16)
        for s in range(1, ndp):
            exchange(sendp, recvp, x_s, x_r, s, q).start()
        recvp[slab(d), cols] = sendp[slab(d), cols]
    loop(CHUNKS, send_tokens)
    for load in loads:
        load.start()
    prod[ndown] = jnp.zeros(prod.shape[1:], f32)

    def take(o, q, sign):
        ag_copy(o, q, twin, o).wait_recv()
        beyond = z - sign

        @pl.when((beyond >= 0) & (beyond < n))
        def _():
            ag_copy(o, q, m - 2 * sign, o).start()
        twin_copy(o, q).start()

    def take_all(tau, q, passing):
        for sign in (-1, 1):
            o, beyond = z + sign * tau, z - sign
            inside = (beyond >= 0) & (beyond < n)
            wanted = inside if passing else jnp.logical_not(inside)

            @pl.when((o >= 0) & (o < n) & wanted)
            def _():
                take(o, q, sign)

    def spread(q):
        cols = cols_of(q)
        for s in range(1, ndp):
            arrived(sendp, recvp, x_s, x_r, s, q).wait_recv()
        mine[z, :, cols] = jnp.dot(compact, recvp[:, cols], preferred_element_type=f32).astype(bf16)

        @pl.when(z < n - 1)
        def _():
            ag_copy(z, q, m + 2, z).start()

        @pl.when(z > 0)
        def _():
            ag_copy(z, q, m - 2, n).start()
        twin_copy(z, q).start()
    loop(CHUNKS, spread)
    for load in loads:
        load.wait()

    def hop(tau, q):
        cols = cols_of(q)

        def pass_on(t, has_more, slot_in, mp):
            part_copy(t, q).wait_recv()
            acc = part[t, :, cols].astype(f32) + sibin[t, :, cols].astype(f32)

            @pl.when(has_more)
            def _():
                rs_copy(t, q, twin, slot_in).wait_recv()
                part[t, :, cols] = (acc + rsin[slot_in, :, cols].astype(f32)).astype(bf16)

            @pl.when(jnp.logical_not(has_more))
            def _():
                part[t, :, cols] = acc.astype(bf16)
            rs_copy(t, q, mp, slot_in).start()

        left = 2 * (n - 1) - z - tau

        @pl.when((left >= 0) & (left < z))
        def _():
            pass_on(left, z < n - 1, left, m - 2)
        right = tau - z

        @pl.when((right > z) & (right < n))
        def _():
            pass_on(right, z > 0, n + right, m + 2)

    def unit(origins, tau, passing):
        rows = pl.ds(0, 2 * bal * len(origins))

        def wait_rows(q):
            for o in origins:
                twin_copy(o, q).wait_recv()
        loop(CHUNKS, wait_rows)
        for i, o in enumerate(origins):
            top = 2 * bal * i
            for b in range(nblk):
                xs[b, top:top + bal, :] = mine[o, :, b * bd:(b + 1) * bd]
                xs[b, top + bal:top + 2 * bal, :] = sib[o, :, b * bd:(b + 1) * bd]

        steps = min(nj, CHUNKS)
        group, passes = nj // steps, CHUNKS // steps

        def columns(g):
            for i in range(group):
                j = g * group + i

                def picked(index):
                    return jnp.concatenate([xs[index[j, k], rows, :] for k in range(knz)], axis=1)
                gv = jnp.dot(picked(gi), gate[j], preferred_element_type=f32)
                uv = jnp.dot(picked(ui), up[j], preferred_element_type=f32)
                hid[j, rows, :] = (gv / (1.0 + jnp.exp(-gv)) * uv).astype(bf16)

            @pl.when(passing)
            def _():
                for i in range(passes):
                    take_all(tau + 1, g * passes + i, True)
        loop(steps, columns)

        def down_row(j):
            h = hid[j, rows, :]
            for i in range(0, knz, 4):
                w = jnp.concatenate([down[j * knz + i + e] for e in range(4)], axis=1)
                p = jnp.dot(h, w, preferred_element_type=f32)
                for e in range(4):
                    prod[j * knz + i + e, rows, :] = p[:, e * bd:(e + 1) * bd]
        loop(nj, down_row)

        def gather(q):
            def some(i):
                for e in range(4):
                    b = q * (nblk // CHUNKS) + 4 * i + e
                    acc = prod[inv[0, b], rows, :]
                    for j in range(1, nj):
                        acc += prod[inv[j, b], rows, :]
                    cols = pl.ds(pl.multiple_of(b * bd, bd), bd)
                    acc = acc.astype(bf16)
                    for r, o in enumerate(origins):
                        top = 2 * bal * r
                        part[o, :, cols] = acc[top:top + bal]
                        sibout[o, :, cols] = acc[top + bal:top + 2 * bal]
            loop(nblk // CHUNKS // 4, some)
            for o in origins:
                part_copy(o, q).start()
        loop(CHUNKS, gather)

    unit([z], 0, z >= 0)

    def phase(i):
        tau = i + 1
        loop(CHUNKS, lambda q: take_all(tau, q, False))

        def side(i):
            o = z + (2 * i - 1) * tau

            @pl.when((o >= 0) & (o < n))
            def _():
                unit([o], tau, (i == 0) | (z - tau < 0))
        loop(2, side)
        loop(CHUNKS, lambda q: hop(tau, q))
    loop(n - 1, phase)

    def finish(q):
        cols = cols_of(q)
        for s in range(1, ndp):
            exchange(sendp, recvp, x_s, x_r, s, q).wait_send()
        part_copy(z, q).wait_recv()
        total[...] = part[z, :, cols].astype(f32) + sibin[z, :, cols].astype(f32)

        @pl.when(z < n - 1)
        def _():
            rs_copy(z, q, twin, z).wait_recv()
            total[...] += rsin[z, :, cols].astype(f32)

        @pl.when(z > 0)
        def _():
            rs_copy(z, q, twin, n + z).wait_recv()
            total[...] += rsin[n + z, :, cols].astype(f32)
        sendp[:, cols] = jnp.dot(expand, total[...].astype(bf16), preferred_element_type=f32).astype(bf16)
        for s in range(1, ndp):
            exchange(sendp, back, bk_s, bk_r, s, q).start()
        back[slab(d), cols] = sendp[slab(d), cols]

    def tail(turn):
        for i in range(n - 2):
            q = turn - i * SKEW

            @pl.when((q >= 0) & (q < CHUNKS))
            def _():
                hop(n + i, q)
        q = turn - (n - 2) * SKEW

        @pl.when(q >= 0)
        def _():
            finish(q)
    loop(CHUNKS + (n - 2) * SKEW, tail)

    def store(q):
        cols = cols_of(q)
        for s in range(1, ndp):
            arrived(sendp, back, bk_s, bk_r, s, q).wait_recv()
        out[:, cols] = jnp.dot(perm_t, back[:, cols], preferred_element_type=f32).astype(bf16)
    loop(CHUNKS, store)

    def drain(q):
        for s in range(1, ndp):
            exchange(sendp, back, bk_s, bk_r, s, q).wait_send()

        @pl.when(z > 0)
        def _():
            ag_copy(z, q, m - 2, n).wait_send()

        def each(o):
            twin_copy(o, q).wait_send()
            part_copy(o, q).wait_send()

            @pl.when(((o <= z) & (z < n - 1)) | ((o > z) & (z > 0)))
            def _():
                ag_copy(o, q, twin, o).wait_send()

            @pl.when(o != z)
            def _():
                rs_copy(o, q, twin, o).wait_send()
        loop(n, each)
    loop(CHUNKS, drain)


def body(tokens, row_counts, gate_blocks, gate_index, up_blocks, up_index, down_blocks, down_index):
    ndp, nmp = lax.axis_size("dp"), lax.axis_size("mp")
    n = nmp // 2
    rows_in, width = tokens.shape
    nj, knz, bd, bf = gate_blocks.shape
    nblk = width // bd
    bal = rows_in // 2
    sl = -(-(rows_in // ndp) // 16) * 16
    ids = jnp.arange(nj * knz, dtype=jnp.int32).reshape(nj, knz)
    hit = down_index[:, :, None] == jnp.arange(nblk, dtype=jnp.int32)
    inv = jnp.min(jnp.where(hit, ids[:, :, None], nj * knz), axis=1)
    bf16 = jnp.bfloat16
    vm, sm, hbm = (pl.BlockSpec(memory_space=s) for s in (pltpu.VMEM, pltpu.SMEM, pl.ANY))
    dma = pltpu.SemaphoreType.DMA
    rows = n * 2 * bal
    tall = 2 * bal
    return pl.pallas_call(
        functools.partial(kernel, ndp, n, sl),
        out_shape=jax.ShapeDtypeStruct(tokens.shape, bf16),
        in_specs=[vm, sm, hbm, sm, hbm, sm, hbm, sm],
        out_specs=vm,
        scratch_shapes=[
            pltpu.VMEM((nj, knz * bd, bf), bf16),
            pltpu.VMEM((nj, knz * bd, bf), bf16),
            pltpu.VMEM((nj * knz, bf, bd), bf16),
            pltpu.VMEM((ndp * sl, width), bf16),
            pltpu.VMEM((ndp * sl, width), bf16),
            pltpu.VMEM((n, bal, width), bf16),
            pltpu.VMEM((n, bal, width), bf16),
            pltpu.VMEM((nblk, tall, bd), bf16),
            pltpu.VMEM((nj, tall, bf), bf16),
            pltpu.VMEM((nj * knz + 1, tall, bd), jnp.float32),
            pltpu.VMEM((bal, width // CHUNKS), jnp.float32),
            pltpu.VMEM((n, bal, width), bf16),
            pltpu.VMEM((n, bal, width), bf16),
            pltpu.VMEM((n, bal, width), bf16),
            pltpu.VMEM((2 * n, bal, width), bf16),
            pltpu.VMEM((ndp * sl, width), bf16),
            dma((3,)),
            dma((ndp - 1, CHUNKS)), dma((ndp - 1, CHUNKS)),
            dma((n + 1, CHUNKS)), dma((n, CHUNKS)),
            dma((n, CHUNKS)), dma((n, CHUNKS)),
            dma((n, CHUNKS)), dma((n, CHUNKS)),
            dma((n, CHUNKS)), dma((2 * n, CHUNKS)),
            dma((ndp - 1, CHUNKS)), dma((ndp - 1, CHUNKS)),
        ],
        compiler_params=pltpu.CompilerParams(
            collective_id=0, has_side_effects=True, vmem_limit_bytes=60 * 1024 * 1024
        ),
        cost_estimate=pl.CostEstimate(
            flops=6 * rows * nj * knz * bd * bf, bytes_accessed=6 * nj * knz * bd * bf, transcendentals=rows * nj * bf
        ),
    )(
        tokens, row_counts, gate_blocks.reshape(nj, knz * bd, bf), gate_index,
        up_blocks.reshape(nj, knz * bd, bf), up_index, down_blocks.reshape(nj * knz, bf, bd), inv,
    )


def solution(mesh):
    in_specs = (
        P(("dp", "mp"), None),
        P(),
        P("mp", None, None, None),
        P("mp", None),
        P("mp", None, None, None),
        P("mp", None),
        P("mp", None, None, None),
        P("mp", None),
    )
    out_specs = P(("dp", "mp"), None)
    return jax.shard_map(body, mesh=mesh, in_specs=in_specs, out_specs=out_specs, check_vma=False)
```

```python
import functools

import jax
import jax.numpy as jnp
from jax import lax
from jax.experimental import pallas as pl
from jax.experimental.pallas import tpu as pltpu
from jax.sharding import PartitionSpec as P

MESH = pl.DeviceIdType.MESH
CHUNKS = 4


def kernel(
    ndp, n, sl,
    tok, cnt, gate_h, gi, up_h, ui, down_h, inv,
    out,
    gate, up, down, sendp, recvp, mine, sib, xs, hid, prod, total, part, sibout, sibin, rsin, back,
    w_sem, x_s, x_r, ag_s, ag_r, sb_s, sb_r, ps_s, ps_r, rs_s, rs_r, bk_s, bk_r,
):
    f32, bf16 = jnp.float32, jnp.bfloat16
    rows_in, width = tok.shape
    bal = mine.shape[1]
    nj, knz = gi.shape
    bf = gate.shape[2]
    bd = down.shape[2]
    nblk = inv.shape[1]
    ndown = down.shape[0]
    chunk = width // CHUNKS
    per_slab = rows_in // ndp
    d, m = lax.axis_index("dp"), lax.axis_index("mp")
    z, c = lax.div(m, 2), lax.rem(m, 2)
    twin = 2 * z + 1 - c

    def cols_of(q):
        return pl.ds(pl.multiple_of(q * chunk, chunk), chunk)

    def slab(s):
        return pl.ds(pl.multiple_of(s * sl, sl), sl)

    def loop(count, fn):
        def step(i, carry):
            fn(i)
            return carry
        lax.fori_loop(0, count, step, 0)

    def remote(src, dst, ssem, rsem, **where):
        return pltpu.make_async_remote_copy(
            src_ref=src, dst_ref=dst, send_sem=ssem, recv_sem=rsem, device_id=where, device_id_type=MESH
        )

    loads = [
        pltpu.make_async_copy(gate_h, gate, w_sem.at[0]),
        pltpu.make_async_copy(up_h, up, w_sem.at[1]),
        pltpu.make_async_copy(down_h, down, w_sem.at[2]),
    ]

    barrier = pltpu.get_barrier_semaphore()
    for s in range(1, ndp):
        pl.semaphore_signal(barrier, inc=1, device_id={"dp": lax.rem(d + s, ndp)}, device_id_type=MESH)
    pl.semaphore_signal(barrier, inc=1, device_id={"mp": twin}, device_id_type=MESH)

    @pl.when(z > 0)
    def _():
        pl.semaphore_signal(barrier, inc=1, device_id={"mp": m - 2}, device_id_type=MESH)

    @pl.when(z < n - 1)
    def _():
        pl.semaphore_signal(barrier, inc=1, device_id={"mp": m + 2}, device_id_type=MESH)

    place = lax.broadcasted_iota(jnp.int32, (ndp * sl, rows_in), 0)
    slot = lax.broadcasted_iota(jnp.int32, (ndp * sl, rows_in), 1)
    inner = lax.rem(place, sl)
    perm = ((slot == inner * ndp + lax.div(place, sl)) & (inner < per_slab)).astype(f32).astype(bf16)
    place_t = lax.broadcasted_iota(jnp.int32, (rows_in, ndp * sl), 1)
    slot_t = lax.broadcasted_iota(jnp.int32, (rows_in, ndp * sl), 0)
    inner_t = lax.rem(place_t, sl)
    perm_t = ((slot_t == inner_t * ndp + lax.div(place_t, sl)) & (inner_t < per_slab)).astype(f32).astype(bf16)

    row = lax.broadcasted_iota(jnp.int32, (bal, ndp * sl), 0)
    col = lax.broadcasted_iota(jnp.int32, (bal, ndp * sl), 1)
    row_t = lax.broadcasted_iota(jnp.int32, (ndp * sl, bal), 1)
    col_t = lax.broadcasted_iota(jnp.int32, (ndp * sl, bal), 0)
    compact = jnp.zeros((bal, ndp * sl), f32)
    expand = jnp.zeros((ndp * sl, bal), f32)
    first = jnp.int32(0)
    for s in range(ndp):
        valid = lax.div(cnt[s, m], ndp)
        low, high = s * sl, s * sl + valid
        compact += ((col >= low) & (col < high) & (row == col - low + first)).astype(f32)
        expand += ((col_t >= low) & (col_t < high) & (row_t == col_t - low + first)).astype(f32)
        first = first + valid
    compact, expand = compact.astype(bf16), expand.astype(bf16)

    def exchange(src, dst, ssem, rsem, s, q):
        peer = lax.rem(d + s, ndp)
        return remote(src.at[slab(peer), cols_of(q)], dst.at[slab(d), cols_of(q)],
                      ssem.at[s - 1, q], rsem.at[s - 1, q], dp=peer)

    def arrived(src, dst, ssem, rsem, s, q):
        peer = lax.rem(d + ndp - s, ndp)
        return remote(src.at[slab(peer), cols_of(q)], dst.at[slab(peer), cols_of(q)],
                      ssem.at[s - 1, q], rsem.at[s - 1, q], dp=peer)

    def ag_copy(o, q, mp, send_slot):
        ref = mine.at[o, :, cols_of(q)]
        return remote(ref, ref, ag_s.at[send_slot, q], ag_r.at[o, q], mp=mp)

    def twin_copy(o, q):
        return remote(mine.at[o, :, cols_of(q)], sib.at[o, :, cols_of(q)], sb_s.at[o, q], sb_r.at[o, q], mp=twin)

    def part_copy(o, q):
        return remote(sibout.at[o, :, cols_of(q)], sibin.at[o, :, cols_of(q)], ps_s.at[o, q], ps_r.at[o, q], mp=twin)

    def rs_copy(t, q, mp, dst_slot):
        return remote(part.at[t, :, cols_of(q)], rsin.at[dst_slot, :, cols_of(q)],
                      rs_s.at[t, q], rs_r.at[dst_slot, q], mp=mp)

    at_end = (z == 0) | (z == n - 1)

    @pl.when(at_end)
    def _():
        pl.semaphore_wait(barrier, ndp + min(n - 1, 1))

    @pl.when(jnp.logical_not(at_end))
    def _():
        pl.semaphore_wait(barrier, ndp + 2)

    def send_tokens(q):
        cols = cols_of(q)
        sendp[:, cols] = jnp.dot(perm, tok[:, cols], preferred_element_type=f32).astype(bf16)
        for s in range(1, ndp):
            exchange(sendp, recvp, x_s, x_r, s, q).start()
        recvp[slab(d), cols] = sendp[slab(d), cols]
    loop(CHUNKS, send_tokens)
    for load in loads:
        load.start()
    prod[ndown] = jnp.zeros(prod.shape[1:], f32)

    def take(o, q, sign):
        ag_copy(o, q, twin, o).wait_recv()
        beyond = z - sign

        @pl.when((beyond >= 0) & (beyond < n))
        def _():
            ag_copy(o, q, m - 2 * sign, o).start()
        twin_copy(o, q).start()

    def take_all(tau, q, passing):
        for sign in (-1, 1):
            o, beyond = z + sign * tau, z - sign
            inside = (beyond >= 0) & (beyond < n)
            wanted = inside if passing else jnp.logical_not(inside)

            @pl.when((o >= 0) & (o < n) & wanted)
            def _():
                take(o, q, sign)

    def spread(q):
        cols = cols_of(q)
        for s in range(1, ndp):
            arrived(sendp, recvp, x_s, x_r, s, q).wait_recv()
        mine[z, :, cols] = jnp.dot(compact, recvp[:, cols], preferred_element_type=f32).astype(bf16)

        @pl.when(z < n - 1)
        def _():
            ag_copy(z, q, m + 2, z).start()

        @pl.when(z > 0)
        def _():
            ag_copy(z, q, m - 2, n).start()
        twin_copy(z, q).start()
    loop(CHUNKS, spread)
    for load in loads:
        load.wait()

    def hop(tau, q):
        cols = cols_of(q)

        def pass_on(t, has_more, slot_in, mp):
            part_copy(t, q).wait_recv()
            acc = part[t, :, cols].astype(f32) + sibin[t, :, cols].astype(f32)

            @pl.when(has_more)
            def _():
                rs_copy(t, q, twin, slot_in).wait_recv()
                part[t, :, cols] = (acc + rsin[slot_in, :, cols].astype(f32)).astype(bf16)

            @pl.when(jnp.logical_not(has_more))
            def _():
                part[t, :, cols] = acc.astype(bf16)
            rs_copy(t, q, mp, slot_in).start()

        left = 2 * (n - 1) - z - tau

        @pl.when((left >= 0) & (left < z))
        def _():
            pass_on(left, z < n - 1, left, m - 2)
        right = tau - z

        @pl.when((right > z) & (right < n))
        def _():
            pass_on(right, z > 0, n + right, m + 2)

    def unit(origins, tau, last):
        rows = pl.ds(0, 2 * bal * len(origins))

        def wait_rows(q):
            for o in origins:
                twin_copy(o, q).wait_recv()
        loop(CHUNKS, wait_rows)
        for i, o in enumerate(origins):
            top = 2 * bal * i
            for b in range(nblk):
                xs[b, top:top + bal, :] = mine[o, :, b * bd:(b + 1) * bd]
                xs[b, top + bal:top + 2 * bal, :] = sib[o, :, b * bd:(b + 1) * bd]

        steps = min(nj, CHUNKS)
        group, passes = nj // steps, CHUNKS // steps

        def columns(g):
            for i in range(group):
                j = g * group + i

                def picked(index):
                    return jnp.concatenate([xs[index[j, k], rows, :] for k in range(knz)], axis=1)
                gv = jnp.dot(picked(gi), gate[j], preferred_element_type=f32)
                uv = jnp.dot(picked(ui), up[j], preferred_element_type=f32)
                hid[j, rows, :] = (gv / (1.0 + jnp.exp(-gv)) * uv).astype(bf16)

            @pl.when(last)
            def _():
                for i in range(passes):
                    take_all(tau + 1, g * passes + i, True)
        loop(steps, columns)

        def down_row(j):
            h = hid[j, rows, :]
            for i in range(0, knz, 2):
                w = jnp.concatenate([down[j * knz + i + e] for e in range(2)], axis=1)
                p = jnp.dot(h, w, preferred_element_type=f32)
                for e in range(2):
                    prod[j * knz + i + e, rows, :] = p[:, e * bd:(e + 1) * bd]
        loop(nj, down_row)

        def gather(q):
            def some(i):
                for e in range(2):
                    b = q * (nblk // CHUNKS) + 2 * i + e
                    acc = prod[inv[0, b], rows, :]
                    for j in range(1, nj):
                        acc += prod[inv[j, b], rows, :]
                    cols = pl.ds(pl.multiple_of(b * bd, bd), bd)
                    acc = acc.astype(bf16)
                    for r, o in enumerate(origins):
                        top = 2 * bal * r
                        part[o, :, cols] = acc[top:top + bal]
                        sibout[o, :, cols] = acc[top + bal:top + 2 * bal]
            loop(nblk // CHUNKS // 2, some)
            for o in origins:
                part_copy(o, q).start()
        loop(CHUNKS, gather)

    unit([z], 0, z >= 0)

    def phase(i):
        tau = i + 1
        loop(CHUNKS, lambda q: take_all(tau, q, False))

        def side(i):
            o = z + (2 * i - 1) * tau

            @pl.when((o >= 0) & (o < n))
            def _():
                unit([o], tau, (i == 1) | (z + tau >= n))
        loop(2, side)
        loop(CHUNKS, lambda q: hop(tau, q))
    loop(n - 1, phase)

    def finish(q):
        cols = cols_of(q)
        for s in range(1, ndp):
            exchange(sendp, recvp, x_s, x_r, s, q).wait_send()
        part_copy(z, q).wait_recv()
        total[...] = part[z, :, cols].astype(f32) + sibin[z, :, cols].astype(f32)

        @pl.when(z < n - 1)
        def _():
            rs_copy(z, q, twin, z).wait_recv()
            total[...] += rsin[z, :, cols].astype(f32)

        @pl.when(z > 0)
        def _():
            rs_copy(z, q, twin, n + z).wait_recv()
            total[...] += rsin[n + z, :, cols].astype(f32)
        sendp[:, cols] = jnp.dot(expand, total[...].astype(bf16), preferred_element_type=f32).astype(bf16)
        for s in range(1, ndp):
            exchange(sendp, back, bk_s, bk_r, s, q).start()
        back[slab(d), cols] = sendp[slab(d), cols]

    def tail(turn):
        for i in range(n - 2):
            q = turn - i

            @pl.when((q >= 0) & (q < CHUNKS))
            def _():
                hop(n + i, q)
        q = turn - (n - 2)

        @pl.when(q >= 0)
        def _():
            finish(q)
    loop(CHUNKS + n - 2, tail)

    def store(q):
        cols = cols_of(q)
        for s in range(1, ndp):
            arrived(sendp, back, bk_s, bk_r, s, q).wait_recv()
        out[:, cols] = jnp.dot(perm_t, back[:, cols], preferred_element_type=f32).astype(bf16)
    loop(CHUNKS, store)

    def drain(q):
        for s in range(1, ndp):
            exchange(sendp, back, bk_s, bk_r, s, q).wait_send()

        @pl.when(z > 0)
        def _():
            ag_copy(z, q, m - 2, n).wait_send()

        def each(o):
            twin_copy(o, q).wait_send()
            part_copy(o, q).wait_send()

            @pl.when(((o <= z) & (z < n - 1)) | ((o > z) & (z > 0)))
            def _():
                ag_copy(o, q, twin, o).wait_send()

            @pl.when(o != z)
            def _():
                rs_copy(o, q, twin, o).wait_send()
        loop(n, each)
    loop(CHUNKS, drain)


def body(tokens, row_counts, gate_blocks, gate_index, up_blocks, up_index, down_blocks, down_index):
    ndp, nmp = lax.axis_size("dp"), lax.axis_size("mp")
    n = nmp // 2
    rows_in, width = tokens.shape
    nj, knz, bd, bf = gate_blocks.shape
    nblk = width // bd
    bal = rows_in // 2
    sl = -(-(rows_in // ndp) // 16) * 16
    ids = jnp.arange(nj * knz, dtype=jnp.int32).reshape(nj, knz)
    hit = down_index[:, :, None] == jnp.arange(nblk, dtype=jnp.int32)
    inv = jnp.min(jnp.where(hit, ids[:, :, None], nj * knz), axis=1)
    bf16 = jnp.bfloat16
    vm, sm, hbm = (pl.BlockSpec(memory_space=s) for s in (pltpu.VMEM, pltpu.SMEM, pl.ANY))
    dma = pltpu.SemaphoreType.DMA
    rows = n * 2 * bal
    tall = 2 * bal
    return pl.pallas_call(
        functools.partial(kernel, ndp, n, sl),
        out_shape=jax.ShapeDtypeStruct(tokens.shape, bf16),
        in_specs=[vm, sm, hbm, sm, hbm, sm, hbm, sm],
        out_specs=vm,
        scratch_shapes=[
            pltpu.VMEM((nj, knz * bd, bf), bf16),
            pltpu.VMEM((nj, knz * bd, bf), bf16),
            pltpu.VMEM((nj * knz, bf, bd), bf16),
            pltpu.VMEM((ndp * sl, width), bf16),
            pltpu.VMEM((ndp * sl, width), bf16),
            pltpu.VMEM((n, bal, width), bf16),
            pltpu.VMEM((n, bal, width), bf16),
            pltpu.VMEM((nblk, tall, bd), bf16),
            pltpu.VMEM((nj, tall, bf), bf16),
            pltpu.VMEM((nj * knz + 1, tall, bd), jnp.float32),
            pltpu.VMEM((bal, width // CHUNKS), jnp.float32),
            pltpu.VMEM((n, bal, width), bf16),
            pltpu.VMEM((n, bal, width), bf16),
            pltpu.VMEM((n, bal, width), bf16),
            pltpu.VMEM((2 * n, bal, width), bf16),
            pltpu.VMEM((ndp * sl, width), bf16),
            dma((3,)),
            dma((ndp - 1, CHUNKS)), dma((ndp - 1, CHUNKS)),
            dma((n + 1, CHUNKS)), dma((n, CHUNKS)),
            dma((n, CHUNKS)), dma((n, CHUNKS)),
            dma((n, CHUNKS)), dma((n, CHUNKS)),
            dma((n, CHUNKS)), dma((2 * n, CHUNKS)),
            dma((ndp - 1, CHUNKS)), dma((ndp - 1, CHUNKS)),
        ],
        compiler_params=pltpu.CompilerParams(
            collective_id=0, has_side_effects=True, vmem_limit_bytes=60 * 1024 * 1024
        ),
        cost_estimate=pl.CostEstimate(
            flops=6 * rows * nj * knz * bd * bf, bytes_accessed=6 * nj * knz * bd * bf, transcendentals=rows * nj * bf
        ),
    )(
        tokens, row_counts, gate_blocks.reshape(nj, knz * bd, bf), gate_index,
        up_blocks.reshape(nj, knz * bd, bf), up_index, down_blocks.reshape(nj * knz, bf, bd), inv,
    )


def solution(mesh):
    in_specs = (
        P(("dp", "mp"), None),
        P(),
        P("mp", None, None, None),
        P("mp", None),
        P("mp", None, None, None),
        P("mp", None),
        P("mp", None, None, None),
        P("mp", None),
    )
    out_specs = P(("dp", "mp"), None)
    return jax.shard_map(body, mesh=mesh, in_specs=in_specs, out_specs=out_specs, check_vma=False)
```
